128 devices in a mesh: col: 8 (over x, y_lo), row: 8 (over z, core), sec: 2 (over y_hi).
Axes of the slice: x: 4, y: 4 (y_hi: 2, y_lo: 2; y = y_hi * 2 + y_lo), z: 4, core: 2. Of those that a mesh axis runs over, the one named last changes fastest.
Arguments:
- corner_left: bfloat16 [8, 8, 256, 256], P('col', 'row'), may hold values from -6 to 6
- corner_right: bfloat16 [8, 8, 256, 256], P('col', 'row'), may hold values from -6 to 6
- edge_top: bfloat16 [8, 8, 256, 100, 256], P('col', 'row', None, 'sec'), may hold values from -0.375 to 0.375
- proj_left: bfloat16 [8, 8, 256, 100, 256], P('col', 'row', None, 'sec')
- proj_right: bfloat16 [8, 8, 100, 256, 256], P('col', 'row', 'sec')
- row_order: int32 [8, 8, 2, 12800], P('col', 'row', 'sec'), may hold values from 0 to 12799, each once within a row
- block_size: int32 [8, 8, 2, 128], P('col', 'row', 'sec'), may hold values from 1 to 128, 12800 in all within a row
- block_sector: int32 [8, 8, 2, 128, 1], P('col', 'row', 'sec'), may hold values from 0 to 15; in each aligned block of 128 rows (0 to 127, 128 to 255, ..., all dimensions but the last counted through in order) at most 12 rows name the same one
- sector_owner: int32 [16], replicated, may hold values from 0 to 15, each once
Outputs:
- new_left: float32 [8, 8, 256, 256], P('col', 'row')
- new_right: float32 [8, 8, 256, 256], P('col', 'row')
- sector_gram: float32 [8, 16, 256, 256], P('col', ('row', 'sec'))
The draws below stay inside these ranges and needn't reach their ends.
Inputs may be any that keep to these rules, and one draw needn't show every extreme that they name: `block_sector`: within the rows of one device (one site and part) no sector has more than 12 blocks, and some sector has exactly 12. `block_size`: sizes of a part's blocks sum to 12800. `row_order`: each part's rows appear once. `sector_owner`: each owner holds one sector.
All inputs are finite; a program needn't handle non-finite values.
Results may differ from the reference program's by a relative error of at most 0.0029.
Values may be sent and summed in bfloat16 or wider, within the bound.
A program may use at most 192 MiB of HBM per device.

```python
import math
import jax
import jax.numpy as jnp
import numpy as np
from jax import lax

CHI = 256
D2 = 100
BLK = 128
NB = 128
LX = 8
LY = 8
NSEC = 16
ROWS_LOC = 12800
CAP = 12
N_SEC = 2


def column_scales(key, count):
    ramp = jnp.arange(count, dtype=jnp.float32) / (count - 1)
    return jnp.exp(math.log(10.0) * ramp)


def draw_proj_left(key, part):
    key = jax.random.fold_in(key, 11)
    noise_key, scale_key = jax.random.split(key)
    shape = (LX, LY, CHI, D2, CHI)
    values = jax.random.normal(noise_key, shape, jnp.float32)
    scales = column_scales(scale_key, CHI)
    return (values * scales / math.sqrt(CHI * D2)).astype(jnp.bfloat16)


def draw_proj_right(key, part):
    key = jax.random.fold_in(key, 12)
    noise_key, scale_key = jax.random.split(key)
    shape = (LX, LY, D2, CHI, CHI)
    values = jax.random.normal(noise_key, shape, jnp.float32)
    scales = column_scales(scale_key, CHI)
    return (values * scales / math.sqrt(CHI * D2)).astype(jnp.bfloat16)


def shard_levels(stream_key, extent, pieces, least, largest):
    def one(dim, shards_of):
        steps = jax.random.uniform(jax.random.fold_in(jax.random.fold_in(stream_key, 6), dim), (shards_of,), jnp.float32, least / len(pieces), largest / len(pieces))
        return jnp.repeat(jnp.exp(steps), extent[dim] // shards_of).reshape((-1,) + (1,) * (len(extent) - dim - 1))

    gain = one(*pieces[0])
    for cut in pieces[1:]:
        gain = gain * one(*cut)
    return gain


def profile(amount, total, bound, slope):
    loads = [(1 << 20) // math.isqrt(rank ** slope) + 1 for rank in range(2, amount + 1)]
    surplus, given = total - bound - (amount - 1), [1] * (amount - 1)
    while surplus > 0:
        candidates = [i for i in range(amount - 1) if given[i] < bound]
        pool, left = sum([loads[i] for i in candidates]), surplus
        for i in candidates:
            addition = min(bound - given[i], max(1, left * loads[i] // pool), surplus)
            given[i] = given[i] + addition
            surplus = surplus - addition
    return np.array([bound] + given)


def uneven_parts(stream_key, number_of, total, reach, slope):
    if number_of == 2:
        one = jax.random.randint(stream_key, (), max(1, total - reach), min(reach, total - 1) + 1)
        return jnp.stack([one, total - one])
    sizes = jnp.asarray(profile(number_of, total, reach, slope), jnp.int32)
    pairs = (number_of - 1) // 2
    giver, receiver = sizes[1:1 + 2 * pairs:2], sizes[2:2 + 2 * pairs:2]
    slack = jnp.minimum(giver - 1, reach - receiver)
    moved = jax.random.randint(jax.random.fold_in(stream_key, 1), (pairs,), 0, 1 << 20) % (slack + 1)
    sizes = sizes.at[1:1 + 2 * pairs:2].set(giver - moved).at[2:2 + 2 * pairs:2].set(receiver + moved)
    return sizes[jax.random.permutation(jax.random.fold_in(stream_key, 2), number_of)]


def routed_block(key, own, number, rows, count, top, limit, skew):
    order = jax.random.permutation(key, count)
    packed, common = load_shares(count, rows * top, limit, skew, True), load_shares(count, rows * top, limit, skew, False)
    places = jnp.arange(count)

    def named(sizes, offset_by):
        used = int((sizes > 0).sum())
        fixed = max(1, used // 4)
        passed = fixed + (places - fixed + offset_by * (used - fixed)) % max(1, count - fixed)
        return jnp.zeros((count,), jnp.int32).at[order[jnp.where(places < fixed, places, passed)]].set(jnp.asarray(sizes, jnp.int32))

    sizes = jnp.where(number % 4 == 0, named(packed, number // 4), named(common, number - number // 4 - 1))
    mixed = jax.random.permutation(jax.random.fold_in(own, 3), count)
    giver, receiver = mixed[0:count // 2 * 2:2], mixed[1:count // 2 * 2:2]
    slack = jnp.minimum(sizes[giver] - 1, limit - sizes[receiver]) // 2
    slack = jnp.where((giver == order[0]) | (receiver == order[0]) | (sizes[receiver] == 0), 0, jnp.maximum(slack, 0))
    passed = jax.random.randint(jax.random.fold_in(own, 4), (count // 2,), 0, 1 << 20) % (slack + 1)
    sizes = sizes.at[giver].add(-passed).at[receiver].add(passed)
    labels = jnp.searchsorted(jnp.cumsum(sizes), jnp.arange(rows * top), side="right").astype(jnp.int32)
    grid = labels.reshape(top, rows).T
    grid = grid[jax.random.permutation(jax.random.fold_in(own, 1), rows)]
    offset_by = jax.random.randint(jax.random.fold_in(own, 2), (rows, 1), 0, top)
    return jnp.take_along_axis(grid, (jnp.arange(top)[None, :] + offset_by) % top, axis=1)


def load_shares(count, total, reach, lean, full):
    weights = [(1 << 20) // math.isqrt(grade ** lean) + 1 for grade in range(1, count + 1)]
    largest = reach if full else min(reach, max(-(-total // count), total * weights[0] // sum(weights)))
    least = 1 if total - largest >= count - 1 else 0
    holding, spare = [largest] + [least] * (count - 1), total - largest - least * (count - 1)
    while spare > 0:
        free = [i for i in range(1, count) if holding[i] < largest] or [i for i in range(1, count) if holding[i] < reach]
        mass, left = sum([weights[i] for i in free]), spare
        for i in free:
            more = min(reach - holding[i], max(1, left * weights[i] // mass), spare)
            holding[i] = holding[i] + more
            spare = spare - more
    return np.array(holding)


def centred(key, extent, deviation, most, cuts=(), kind=jnp.bfloat16):
    factor_of = shard_levels(key, extent, cuts, -0.22, 0.18) if cuts else 1.0
    array = jax.random.normal(key, extent, jnp.float32) * deviation * factor_of
    return jnp.minimum(jnp.maximum(array, -most), most).astype(kind)


def setup_inputs(seed: int = 0) -> dict:
    key_list = jax.random.split(jax.random.key(seed), 10)
    corner_left = centred(key_list[0], (LX, LY, CHI, CHI), 1.0, 6.0, ((0, 8), (1, 8)))
    corner_right = centred(key_list[1], (LX, LY, CHI, CHI), 1.0, 6.0, ((0, 8), (1, 8)))
    edge_top = centred(key_list[2], (LX, LY, CHI, D2, CHI), CHI ** -0.5, 0.375, ((0, 8), (1, 8), (3, 2)))
    proj_left = draw_proj_left(jax.random.fold_in(key_list[9], 71), 0)
    proj_right = draw_proj_right(jax.random.fold_in(key_list[9], 71), 0)
    row_order = jax.vmap(lambda own: jax.random.permutation(own, ROWS_LOC))(jax.random.split(key_list[5], LX * LY * N_SEC)).reshape((LX, LY, N_SEC, ROWS_LOC)).astype(jnp.int32)
    block_size = jax.vmap(lambda own: uneven_parts(own, NB, ROWS_LOC, BLK, 1))(jax.random.split(key_list[6], LX * LY * N_SEC)).reshape((LX, LY, N_SEC, NB)).astype(jnp.int32)
    block_sector_keys = jax.random.split(jax.random.fold_in(key_list[7], 1), LX * LY * N_SEC * NB // NB)
    block_sector_turns = jax.random.permutation(jax.random.fold_in(key_list[7], 3), LX * LY * N_SEC * NB // NB)
    block_sector = jax.vmap(lambda own, number: routed_block(jax.random.fold_in(key_list[7], 2), own, number, NB, NSEC, 1, CAP, 2))(block_sector_keys, block_sector_turns).reshape((LX, LY, N_SEC, NB, 1))
    sector_owner = jax.random.permutation(key_list[8], NSEC).astype(jnp.int32)
    return {"corner_left": corner_left, "corner_right": corner_right, "edge_top": edge_top, "proj_left": proj_left, "proj_right": proj_right, "row_order": row_order, "block_size": block_size, "block_sector": block_sector, "sector_owner": sector_owner}


epsilon = 1e-06

def normalize(raw_corner):
    return raw_corner * lax.rsqrt(jnp.mean(raw_corner * raw_corner) + epsilon)

def block_rows(part_rows, row_perm, lengths):
    starts = (jnp.cumsum(lengths) - lengths).astype(jnp.int32)
    offsets = jnp.arange(BLK, dtype=jnp.int32)
    position = jnp.minimum(starts[:, None] + offsets[None, :], ROWS_LOC - 1).astype(jnp.int32)
    usable = offsets[None, :] < lengths[:, None]
    picked = jnp.take(part_rows, jnp.take(row_perm, position).astype(jnp.int32), axis=0)
    return jnp.where(usable[:, :, None], picked, jnp.zeros_like(picked))

def site_terms(from_left, from_right, top_edge, left_proj, right_proj, row_perm, lengths, sectors):
    joined_rows = CHI * D2
    enlarged = jnp.dot(from_left, top_edge.reshape(CHI, joined_rows), preferred_element_type=jnp.float32).astype(jnp.bfloat16)
    left_raw = lax.dot_general(left_proj.reshape(joined_rows, CHI), enlarged.reshape(joined_rows, CHI), (((0,), (0,)), ((), ())), preferred_element_type=jnp.float32)
    right_big = jnp.dot(top_edge.reshape(joined_rows, CHI), from_right, preferred_element_type=jnp.float32).astype(jnp.bfloat16)
    right_raw = jnp.dot(right_big.reshape(CHI, joined_rows), right_proj.reshape(joined_rows, CHI), preferred_element_type=jnp.float32)
    halves = enlarged.reshape(CHI, N_SEC, D2 // N_SEC, CHI)
    sector_sums = jnp.zeros((NSEC, CHI, CHI), jnp.float32)
    for sec_part in range(N_SEC):
        part_rows = halves[:, sec_part].reshape(ROWS_LOC, CHI)
        picked = block_rows(part_rows, row_perm[sec_part], lengths[sec_part]).astype(jnp.float32)
        block_grams = jnp.einsum('kra,krb->kab', picked, picked, precision=lax.Precision.HIGHEST)
        onehot = (sectors[sec_part][None, :] == jnp.arange(NSEC, dtype=jnp.int32)[:, None]).astype(jnp.float32)
        sector_sums = sector_sums + jnp.einsum('sk,kab->sab', onehot, block_grams, precision=lax.Precision.HIGHEST)
    return (normalize(left_raw), normalize(right_raw), sector_sums)

def reference(corner_left, corner_right, edge_top, proj_left, proj_right, row_order, block_size, block_sector, sector_owner):
    shifted_left = jnp.roll(corner_left, 1, axis=0)
    shifted_right = jnp.roll(corner_right, -1, axis=0)

    def column(column_id):

        def one_row(carried, row_id):
            left_new, right_new, sector_sums = site_terms(shifted_left[column_id, row_id], shifted_right[column_id, row_id], edge_top[column_id, row_id], proj_left[column_id, row_id], proj_right[column_id, row_id], row_order[column_id, row_id], block_size[column_id, row_id], block_sector[column_id, row_id, :, :, 0])
            return (carried + sector_sums, (left_new, right_new))
        totals, corners = lax.scan(one_row, jnp.zeros((NSEC, CHI, CHI), jnp.float32), jnp.arange(LY, dtype=jnp.int32))
        by_owner = jnp.zeros_like(totals).at[sector_owner].set(totals)
        return (corners[0], corners[1], by_owner)
    new_left, new_right, sector_gram = lax.map(column, jnp.arange(LX, dtype=jnp.int32))
    return (new_left, new_right, sector_gram)
```

```python
import functools

import jax
import jax.numpy as jnp
from jax import lax
from jax.experimental import pallas as pl
from jax.experimental.pallas import tpu as pltpu
from jax.sharding import PartitionSpec as P

CHI = 256
UNITS = 50
OWNERS = 16
LANES = 128
TILE = 16
TILES = 32
CAP_TILES = 144
DUMP = OWNERS * CAP_TILES
GROUP = 5
GRAM_TILES = 48
EPSILON = 1e-06

F32 = jnp.float32
BF16 = jnp.bfloat16


def dot(x, y):
    return lax.dot_general(x, y, (((1,), (0,)), ((), ())), preferred_element_type=F32)


def dot_nt(x, y):
    return lax.dot_general(x, y, (((1,), (1,)), ((), ())), preferred_element_type=F32)


def dot_tn(x, y):
    return lax.dot_general(x, y, (((0,), (0,)), ((), ())), preferred_element_type=F32)


def iota(shape, axis):
    return lax.broadcasted_iota(jnp.int32, shape, axis)


def ones_where(mask):
    return jnp.where(mask, 1.0, 0.0).astype(BF16)


def plan_kernel(owner_ref, order_ref, size_ref, sector_ref, dest_ref, place_ref, count_ref):
    sector = sector_ref[...]
    named = jnp.zeros((1, LANES), F32)
    for s in range(OWNERS):
        named = jnp.where(sector == s, (owner_ref[s] + 1).astype(F32), named)
    up = iota((LANES, LANES), 0)
    across = iota((LANES, LANES), 1)
    before = ones_where(up < across)
    steps = ones_where(up == across) - ones_where(up + 1 == across)
    sizes = jnp.broadcast_to(size_ref[...].astype(F32), (8, LANES)).astype(BF16)
    starts = dot(sizes, before)[0:1]
    delta = dot(jnp.broadcast_to(named, (8, LANES)).astype(BF16), steps)[0:1]
    start_hi = jnp.floor((starts + 0.5) * (1.0 / LANES))
    start_lo = starts - LANES * start_hi
    place_hi = iota((104, LANES), 0).astype(F32)
    impulses = dot_nt(
        jnp.where(place_hi == start_hi, delta, 0.0).astype(BF16),
        ones_where(up.astype(F32) == start_lo),
    ).astype(BF16)
    inside = dot(impulses, ones_where(up <= across))
    totals = jnp.broadcast_to(inside[:, LANES - 1:LANES], (104, LANES)).astype(BF16)
    earlier = ones_where(iota((104, 104), 1) < iota((104, 104), 0))
    listed = inside + dot(earlier, totals)
    order = order_ref[...].astype(F32)
    bond = jnp.floor((order + 0.5) * (1.0 / UNITS))
    unit = order - UNITS * bond
    bonds = iota((CHI, LANES), 0).astype(F32)
    units = iota((64, LANES), 0).astype(F32)
    owned = jnp.zeros((64, CHI), F32)
    for first in range(0, 100, 10):
        left, right = [], []
        for h in range(first, first + 10):
            left.append(jnp.where(units == unit[h:h + 1], listed[h:h + 1], 0.0).astype(BF16))
            right.append(ones_where(bonds == bond[h:h + 1]))
        owned = owned + dot_nt(jnp.concatenate(left, axis=1), jnp.concatenate(right, axis=1))
    hits = [owned == float(o + 1) for o in range(OWNERS)]
    onehot = [ones_where(hit) for hit in hits]
    lower = ones_where(iota((CHI, CHI), 0) < iota((CHI, CHI), 1))
    offset = jnp.zeros((64, 1), F32)
    dest = jnp.full((64, CHI), -1.0, F32)
    lane = iota((64, LANES), 1)
    tile_counts = jnp.zeros((64, LANES), F32)
    offsets, counts = [], []
    for o in range(OWNERS):
        rank = dot(onehot[o], lower)
        amount = rank[:, CHI - 1:CHI] + onehot[o].astype(F32)[:, CHI - 1:CHI]
        tiles = jnp.floor((amount + (TILE - 1)) * (1.0 / TILE))
        dest = jnp.where(hits[o], TILE * offset + rank, dest)
        tile_counts = jnp.where(lane == o, tiles, tile_counts)
        offsets.append(offset)
        counts.append(tiles)
        offset = offset + tiles
    dest_ref[...] = dest
    earlier = ones_where(iota((64, 64), 1) < iota((64, 64), 0))
    sofar = dot(earlier, tile_counts.astype(BF16))
    slot = lane.astype(F32)
    place = jnp.full((64, LANES), float(DUMP), F32)
    for o in range(OWNERS):
        mine = (slot >= offsets[o]) & (slot < offsets[o] + counts[o])
        place = jnp.where(mine, sofar[:, o:o + 1] - offsets[o] + slot + float(o * CAP_TILES), place)
    place_ref[...] = place.astype(jnp.int32)
    count_ref[...] = jnp.sum(tile_counts, axis=0, keepdims=True).astype(jnp.int32)


def plan(sector_owner, row_order, block_size, block_sector):
    vmem = pl.BlockSpec(memory_space=pltpu.VMEM)
    return pl.pallas_call(
        plan_kernel,
        out_shape=(
            jax.ShapeDtypeStruct((64, CHI), F32),
            jax.ShapeDtypeStruct((64, LANES), jnp.int32),
            jax.ShapeDtypeStruct((1, LANES), jnp.int32),
        ),
        in_specs=[pl.BlockSpec(memory_space=pltpu.SMEM), vmem, vmem, vmem],
        out_specs=(vmem, vmem, vmem),
        cost_estimate=pl.CostEstimate(flops=2 * 64 * 12800 * 256, bytes_accessed=200000, transcendentals=0),
        compiler_params=pltpu.CompilerParams(vmem_limit_bytes=32 * 1024 * 1024),
    )(sector_owner, row_order, block_size, block_sector)


def site_kernel(
    place_ref, count_ref, dest_ref, left_ref, right_ref, edge_ref, proj_left_ref, proj_right_ref,
    out_left, out_right, out_gram, enlarged, wide, buckets,
):
    step = pl.program_id(0)

    @pl.when(step == 0)
    def _():
        out_left[...] = jnp.zeros_like(out_left)
        out_right[...] = jnp.zeros_like(out_right)

    slots = iota((TILES * TILE, CHI), 0).astype(F32)
    for j in range(GROUP):
        rows = pl.ds(j * CHI, CHI)
        enlarged[rows, :] = dot(left_ref[...], edge_ref[j]).astype(BF16)
        wide[:, rows] = dot(edge_ref[j], right_ref[...]).astype(BF16)
    out_left[...] += dot_tn(proj_left_ref[...].reshape(GROUP * CHI, CHI), enlarged[...])
    out_right[...] += dot(wide[...], proj_right_ref[...].reshape(GROUP * CHI, CHI))
    for j in range(GROUP):
        u = step * GROUP + j
        pick = ones_where(slots == dest_ref[pl.ds(u, 1), :])
        sorted_rows = dot(pick, enlarged[pl.ds(j * CHI, CHI), :]).astype(BF16)
        for t in range(TILES - 1):
            at = pl.multiple_of(place_ref[u, t] * TILE, TILE)
            buckets[pl.ds(at, TILE), :] = sorted_rows[t * TILE:(t + 1) * TILE]

    @pl.when(step == UNITS // GROUP - 1)
    def _():
        @pl.loop(0, OWNERS)
        def _(o):
            total = count_ref[0, o]
            products = (total + (GRAM_TILES - 1)) // GRAM_TILES
            base = o * CAP_TILES

            @pl.loop(total, products * GRAM_TILES)
            def _(t):
                at = pl.multiple_of((base + t) * TILE, TILE)
                buckets[pl.ds(at, TILE), :] = jnp.zeros((TILE, CHI), BF16)

            out_gram[o] = jnp.zeros((CHI, CHI), F32)

            @pl.loop(0, products)
            def _(k):
                at = pl.multiple_of((base + k * GRAM_TILES) * TILE, TILE)
                rows = buckets[pl.ds(at, GRAM_TILES * TILE), :]
                out_gram[o] += dot_tn(rows, rows)


def site(place, count, dest, from_left, from_right, edge, proj_left, proj_right):
    whole = lambda shape: pl.BlockSpec(shape, lambda i, *_: (0,) * len(shape))
    group = pl.BlockSpec((GROUP, CHI, CHI), lambda i, *_: (i, 0, 0))
    return pl.pallas_call(
        site_kernel,
        grid_spec=pltpu.PrefetchScalarGridSpec(
            num_scalar_prefetch=2,
            grid=(UNITS // GROUP,),
            in_specs=[whole((64, CHI)), whole((CHI, CHI)), whole((CHI, CHI)), group, group, group],
            out_specs=[whole((CHI, CHI)), whole((CHI, CHI)), whole((OWNERS, CHI, CHI))],
            scratch_shapes=[
                pltpu.VMEM((GROUP * CHI, CHI), BF16),
                pltpu.VMEM((CHI, GROUP * CHI), BF16),
                pltpu.VMEM(((DUMP + 1) * TILE, CHI), BF16),
            ],
        ),
        out_shape=(
            jax.ShapeDtypeStruct((CHI, CHI), F32),
            jax.ShapeDtypeStruct((CHI, CHI), F32),
            jax.ShapeDtypeStruct((OWNERS, CHI, CHI), F32),
        ),
        cost_estimate=pl.CostEstimate(flops=8 * 2 * 12800 * 65536, bytes_accessed=24 << 20, transcendentals=0),
        compiler_params=pltpu.CompilerParams(vmem_limit_bytes=56 * 1024 * 1024),
    )(place, count, dest, from_left, from_right, edge, proj_left, proj_right)


def from_behind(value, axis, steps):
    count = lax.axis_size(axis)
    pairs = [(source, (source + steps) % count) for source in range(count)]
    return lax.ppermute(value, axis, pairs)


def body(
    corner_left, corner_right, edge_top, proj_left, proj_right, row_order, block_size, block_sector, sector_owner,
):
    from_left = from_behind(corner_left, "col", 1)[0, 0]
    from_right = from_behind(corner_right, "col", -1)[0, 0]
    dest, place, count = plan(
        sector_owner,
        row_order.reshape(100, LANES),
        block_size.reshape(1, LANES),
        block_sector.reshape(1, LANES),
    )
    edge = jnp.transpose(edge_top[0, 0], (1, 0, 2))
    left = jnp.transpose(proj_left[0, 0], (1, 0, 2))
    left_part, right_part, grams = site(place, count, dest, from_left, from_right, edge, left, proj_right[0, 0])
    parts = lax.all_to_all(grams.astype(BF16), ("row", "sec"), split_axis=0, concat_axis=0, tiled=True)
    sector_gram = jnp.sum(parts.astype(F32), axis=0)[None, None]
    left_sum, right_sum = lax.psum((left_part, right_part), "sec")
    new_left = left_sum * lax.rsqrt(jnp.mean(left_sum * left_sum) + EPSILON)
    new_right = right_sum * lax.rsqrt(jnp.mean(right_sum * right_sum) + EPSILON)
    return (new_left[None, None], new_right[None, None], sector_gram)


def solution(mesh):
    in_specs = (
        P("col", "row", None, None),
        P("col", "row", None, None),
        P("col", "row", None, "sec", None),
        P("col", "row", None, "sec", None),
        P("col", "row", "sec", None, None),
        P("col", "row", "sec", None),
        P("col", "row", "sec", None),
        P("col", "row", "sec", None, None),
        P(),
    )
    out_specs = (
        P("col", "row", None, None),
        P("col", "row", None, None),
        P("col", ("row", "sec"), None, None),
    )
    return jax.shard_map(body, mesh=mesh, in_specs=in_specs, out_specs=out_specs, check_vma=False)
```

```python
import functools

import jax
import jax.numpy as jnp
from jax import lax
from jax.experimental import pallas as pl
from jax.experimental.pallas import tpu as pltpu
from jax.sharding import PartitionSpec as P

CHI = 256
UNITS = 50
OWNERS = 16
LANES = 128
TILE = 16
TILES = 32
CAP_TILES = 144
EMPTY = TILES - 1
GROUP = 10
STEPS = UNITS // GROUP
HALF = 128
PACKED = 2 * HALF + TILE
Z_CHIPS = 4
EPSILON = 1e-06
MESH = pl.DeviceIdType.MESH

F32 = jnp.float32
BF16 = jnp.bfloat16


def dot(x, y):
    return lax.dot_general(x, y, (((1,), (0,)), ((), ())), preferred_element_type=F32)


def dot_nt(x, y):
    return lax.dot_general(x, y, (((1,), (1,)), ((), ())), preferred_element_type=F32)


def dot_tn(x, y):
    return lax.dot_general(x, y, (((0,), (0,)), ((), ())), preferred_element_type=F32)


def iota(shape, axis):
    return lax.broadcasted_iota(jnp.int32, shape, axis)


def ones_where(mask):
    return jnp.where(mask, 1.0, 0.0).astype(BF16)


def plan_kernel(owner_ref, order_ref, size_ref, sector_ref, dest_ref, tile_ref):
    sector = sector_ref[...]
    named = jnp.zeros((1, LANES), F32)
    for s in range(OWNERS):
        named = jnp.where(sector == s, (owner_ref[s] + 1).astype(F32), named)
    up = iota((LANES, LANES), 0)
    across = iota((LANES, LANES), 1)
    before = ones_where(up < across)
    steps = ones_where(up == across) - ones_where(up + 1 == across)
    sizes = jnp.broadcast_to(size_ref[...].astype(F32), (8, LANES)).astype(BF16)
    starts = dot(sizes, before)[0:1]
    delta = dot(jnp.broadcast_to(named, (8, LANES)).astype(BF16), steps)[0:1]
    start_hi = jnp.floor((starts + 0.5) * (1.0 / LANES))
    start_lo = starts - LANES * start_hi
    place_hi = iota((104, LANES), 0).astype(F32)
    impulses = dot_nt(
        jnp.where(place_hi == start_hi, delta, 0.0).astype(BF16),
        ones_where(up.astype(F32) == start_lo),
    ).astype(BF16)
    inside = dot(impulses, ones_where(up <= across))
    totals = jnp.broadcast_to(inside[:, LANES - 1:LANES], (104, LANES)).astype(BF16)
    earlier = ones_where(iota((104, 104), 1) < iota((104, 104), 0))
    listed = inside + dot(earlier, totals)
    order = order_ref[...].astype(F32)
    bond = jnp.floor((order + 0.5) * (1.0 / UNITS))
    unit = order - UNITS * bond
    bonds = iota((CHI, LANES), 0).astype(F32)
    units = iota((64, LANES), 0).astype(F32)
    owned = jnp.zeros((64, CHI), F32)
    for first in range(0, 100, 10):
        left, right = [], []
        for h in range(first, first + 10):
            left.append(jnp.where(units == unit[h:h + 1], listed[h:h + 1], 0.0).astype(BF16))
            right.append(ones_where(bonds == bond[h:h + 1]))
        owned = owned + dot_nt(jnp.concatenate(left, axis=1), jnp.concatenate(right, axis=1))
    hits = [owned == float(o + 1) for o in range(OWNERS)]
    onehot = [ones_where(hit) for hit in hits]
    lower = ones_where(iota((CHI, CHI), 0) < iota((CHI, CHI), 1))
    offset = jnp.zeros((64, 1), F32)
    dest = jnp.full((64, CHI), -1.0, F32)
    lane = iota((64, LANES), 1)
    tile_counts = jnp.zeros((64, LANES), F32)
    tile_offsets = jnp.zeros((64, LANES), F32)
    for o in range(OWNERS):
        rank = dot(onehot[o], lower)
        amount = rank[:, CHI - 1:CHI] + onehot[o].astype(F32)[:, CHI - 1:CHI]
        tiles = jnp.floor((amount + (TILE - 1)) * (1.0 / TILE))
        dest = jnp.where(hits[o], TILE * offset + rank, dest)
        tile_counts = jnp.where(lane == o, tiles, tile_counts)
        tile_offsets = jnp.where(lane == o, offset, tile_offsets)
        offset = offset + tiles
    dest_ref[...] = dest
    eye = ones_where(iota((OWNERS, LANES), 0) == iota((OWNERS, LANES), 1))
    counts = dot_nt(eye, tile_counts.astype(BF16))
    offsets = dot_nt(eye, tile_offsets.astype(BF16))
    sofar = dot(counts.astype(BF16), ones_where(iota((64, 64), 0) < iota((64, 64), 1)))
    chunk = iota((OWNERS, 64), 1)
    base = offsets - sofar + (chunk * TILES).astype(F32)
    previous = jnp.where(chunk == 0, 0.0, pltpu.roll(base, 1, 1))
    jump = base - previous
    place = iota((OWNERS, CHI), 1).astype(F32)
    tile = place
    for u in range(UNITS):
        tile = tile + jnp.where(place >= sofar[:, u:u + 1], jump[:, u:u + 1], 0.0)
    used = sofar[:, UNITS - 1:UNITS] + counts[:, UNITS - 1:UNITS]
    tile_ref[...] = jnp.where(place < used, tile, float(EMPTY)).astype(jnp.int32)


def plan(sector_owner, row_order, block_size, block_sector):
    vmem = pl.BlockSpec(memory_space=pltpu.VMEM)
    return pl.pallas_call(
        plan_kernel,
        out_shape=(
            jax.ShapeDtypeStruct((64, CHI), F32),
            jax.ShapeDtypeStruct((OWNERS, CHI), jnp.int32),
        ),
        in_specs=[pl.BlockSpec(memory_space=pltpu.SMEM), vmem, vmem, vmem],
        out_specs=(vmem, vmem),
        cost_estimate=pl.CostEstimate(flops=2 * 64 * 12800 * 256, bytes_accessed=200000, transcendentals=0),
        compiler_params=pltpu.CompilerParams(vmem_limit_bytes=32 * 1024 * 1024),
    )(sector_owner, row_order, block_size, block_sector)


def sort_matrix(place):
    place = jnp.broadcast_to(place, (TILE, CHI))
    low = jnp.where(place < CHI, place, -1.0).astype(BF16)
    high = jnp.where(place >= CHI, place - CHI, -1.0).astype(BF16)
    rows = iota((CHI // TILE, TILE, CHI), 0) * TILE + iota((CHI // TILE, TILE, CHI), 1)
    rows = rows.astype(F32).astype(BF16)
    one, zero = jnp.ones((), BF16), jnp.zeros((), BF16)
    return jnp.concatenate(
        [jnp.where(rows == part[None], one, zero).reshape(CHI, CHI) for part in (low, high)], axis=0
    )


def pack(gram):
    upper, corner, lower = gram[:HALF, :HALF], gram[:HALF, HALF:], gram[HALF:, HALF:]
    row, col = iota((HALF, HALF), 0), iota((HALF, HALF), 1)
    diagonal = jnp.sum(jnp.where(row == col, lower, 0.0), axis=0, keepdims=True)
    return jnp.concatenate(
        [jnp.where(row <= col, upper, lower), corner, jnp.broadcast_to(diagonal, (TILE, HALF))], axis=0
    )


def unpack(packed):
    square, corner, diagonal = packed[:HALF], packed[HALF:CHI], packed[CHI:CHI + 1]
    row, col = iota((HALF, HALF), 0), iota((HALF, HALF), 1)
    turned = square.T
    upper = jnp.where(row <= col, square, turned)
    lower = jnp.where(row == col, diagonal, jnp.where(row > col, square, turned))
    return jnp.concatenate(
        [jnp.concatenate([upper, corner], axis=1), jnp.concatenate([corner.T, lower], axis=1)], axis=0
    )


def normalized(total):
    mean = jnp.sum(total * total, keepdims=True) * (1.0 / (CHI * CHI))
    return total * lax.rsqrt(mean + EPSILON)


def column_kernel(
    tile_ref, dest_ref, left_ref, right_ref, edge_hbm, proj_left_hbm, proj_right_hbm,
    out_left, out_right, out_gram,
    edge, proj_left, proj_right, enlarged, wide, sorted_rows, listed,
    left_sum, right_sum, left_other, right_other,
    mine, to_mate, from_mate, to_row, from_row, to_sec, from_sec,
    load_sem, corner_send, corner_recv, mate_send, mate_recv, row_send, row_recv, sec_send, sec_recv,
):
    row, sec = lax.axis_index("row"), lax.axis_index("sec")
    z, core = row // 2, row % 2
    mate = {"row": z * 2 + (1 - core)}
    partner = {"sec": 1 - sec}
    ahead = [{"row": ((z + dz) % Z_CHIPS) * 2 + core} for dz in range(1, Z_CHIPS)]

    barrier = pltpu.get_barrier_semaphore()
    for other in [mate, partner] + ahead:
        pl.semaphore_signal(barrier, inc=1, device_id=other, device_id_type=MESH)

    pairs = ((edge_hbm, edge), (proj_left_hbm, proj_left), (proj_right_hbm, proj_right))

    def load(k, i):
        part = pl.ds(i * GROUP, GROUP)
        return pltpu.make_async_copy(pairs[k][0].at[part], pairs[k][1].at[part], load_sem.at[k, i])

    for i in range(STEPS):
        load(0, i).start()
        load(1, i).start()
    for i in range(STEPS):
        load(2, i).start()

    left_sum[...] = jnp.zeros_like(left_sum)
    right_sum[...] = jnp.zeros_like(right_sum)

    @pl.loop(0, STEPS)
    def _(i):
        load(0, i).wait()
        load(1, i).wait()
        for j in range(GROUP):
            enlarged[pl.ds(j * CHI, CHI), :] = dot(left_ref[...], edge[i * GROUP + j]).astype(BF16)
        chunk = proj_left[pl.ds(i * GROUP, GROUP)].reshape(GROUP * CHI, CHI)
        left_sum[...] += dot_tn(chunk, enlarged[...])
        for j in range(GROUP):
            u = i * GROUP + j
            ordered = dot(sort_matrix(dest_ref[pl.ds(u, 1), :]), enlarged[pl.ds(j * CHI, CHI), :])
            sorted_rows[pl.ds(u * TILES, TILES)] = ordered.astype(BF16).reshape(TILES, TILE, CHI)

    pl.semaphore_wait(barrier, 2 + len(ahead))

    def corner_copy(k):
        source, target = ((left_sum, left_other), (right_sum, right_other))[k]
        return pltpu.make_async_remote_copy(
            src_ref=source, dst_ref=target, send_sem=corner_send.at[k], recv_sem=corner_recv.at[k],
            device_id=partner, device_id_type=MESH,
        )

    corner_copy(0).start()

    @pl.loop(0, STEPS)
    def _(i):
        load(2, i).wait()
        for j in range(GROUP):
            wide[:, pl.ds(j * CHI, CHI)] = dot(edge[i * GROUP + j], right_ref[...]).astype(BF16)
        chunk = proj_right[pl.ds(i * GROUP, GROUP)].reshape(GROUP * CHI, CHI)
        right_sum[...] += dot(wide[...], chunk)

    corner_copy(1).start()

    def owner_gram(k, owner):
        for t in range(CAP_TILES):
            listed[k, pl.ds(t * TILE, TILE), :] = sorted_rows[tile_ref[owner, t]]
        rows = listed[k]
        return pack(dot_tn(rows, rows))

    def mate_copy(i):
        return pltpu.make_async_remote_copy(
            src_ref=to_mate.at[i], dst_ref=from_mate.at[i], send_sem=mate_send.at[i], recv_sem=mate_recv.at[i],
            device_id=mate, device_id_type=MESH,
        )

    def row_copy(j):
        target = {"row": ((z + 1 + j // 2) % Z_CHIPS) * 2 + core}
        return pltpu.make_async_remote_copy(
            src_ref=to_row.at[j], dst_ref=from_row.at[j], send_sem=row_send.at[j], recv_sem=row_recv.at[j],
            device_id=target, device_id_type=MESH,
        )

    sec_copy = pltpu.make_async_remote_copy(
        src_ref=to_sec, dst_ref=from_sec, send_sem=sec_send, recv_sem=sec_recv,
        device_id=partner, device_id_type=MESH,
    )

    @pl.loop(0, 2 * Z_CHIPS)
    def _(i):
        z_owner = (z + 1 + i // 2) % Z_CHIPS
        sec_owner = (sec + 1 + i) % 2
        to_mate[i] = owner_gram(0, z_owner * 4 + (1 - core) * 2 + sec_owner)
        mate_copy(i).start()
        mine[i] = owner_gram(1, z_owner * 4 + core * 2 + sec_owner)

        @pl.when((i >= 1) & (i <= 6))
        def _():
            mate_copy(i - 1).wait_recv()
            to_row[i - 1] = (mine[i - 1] + from_mate[i - 1]).astype(BF16)
            row_copy(i - 1).start()

    def column_sum(r):
        mate_copy(6 + r).wait_recv()
        total = mine[6 + r] + from_mate[6 + r]
        for k in range(Z_CHIPS - 1):
            row_copy(2 * k + r).wait_recv()
            total = total + from_row[2 * k + r].astype(F32)
        return total

    to_sec[...] = column_sum(0).astype(BF16)
    sec_copy.start()
    corner_copy(0).wait()
    out_left[...] = normalized(left_sum[...] + left_other[...])
    corner_copy(1).wait()
    out_right[...] = normalized(right_sum[...] + right_other[...])
    total = column_sum(1)
    sec_copy.wait_recv()
    out_gram[...] = unpack(total + from_sec[...].astype(F32))
    for i in range(2 * Z_CHIPS):
        mate_copy(i).wait_send()
    for j in range(2 * (Z_CHIPS - 1)):
        row_copy(j).wait_send()
    sec_copy.wait_send()


def column(tiles, dest, from_left, from_right, edge, proj_left, proj_right):
    vmem = pl.BlockSpec(memory_space=pltpu.VMEM)
    anywhere = pl.BlockSpec(memory_space=pl.ANY)
    square = jax.ShapeDtypeStruct((CHI, CHI), F32)
    whole = pltpu.VMEM((UNITS, CHI, CHI), BF16)
    dma = pltpu.SemaphoreType.DMA
    return pl.pallas_call(
        column_kernel,
        in_specs=[pl.BlockSpec(memory_space=pltpu.SMEM), vmem, vmem, vmem, anywhere, anywhere, anywhere],
        out_specs=(vmem, vmem, vmem),
        out_shape=(square, square, square),
        scratch_shapes=[
            whole, whole, whole,
            pltpu.VMEM((GROUP * CHI, CHI), BF16),
            pltpu.VMEM((CHI, GROUP * CHI), BF16),
            pltpu.VMEM((UNITS * TILES, TILE, CHI), BF16),
            pltpu.VMEM((2, CAP_TILES * TILE, CHI), BF16),
            pltpu.VMEM((CHI, CHI), F32), pltpu.VMEM((CHI, CHI), F32),
            pltpu.VMEM((CHI, CHI), F32), pltpu.VMEM((CHI, CHI), F32),
            pltpu.VMEM((8, PACKED, HALF), F32),
            pltpu.VMEM((8, PACKED, HALF), F32),
            pltpu.VMEM((8, PACKED, HALF), F32),
            pltpu.VMEM((6, PACKED, HALF), BF16),
            pltpu.VMEM((6, PACKED, HALF), BF16),
            pltpu.VMEM((PACKED, HALF), BF16),
            pltpu.VMEM((PACKED, HALF), BF16),
            dma((3, STEPS)), dma((2,)), dma((2,)), dma((8,)), dma((8,)), dma((6,)), dma((6,)), dma, dma,
        ],
        cost_estimate=pl.CostEstimate(flops=9 * 2 * 12800 * 65536, bytes_accessed=24 << 20, transcendentals=0),
        compiler_params=pltpu.CompilerParams(
            collective_id=0, has_side_effects=True, vmem_limit_bytes=60 * 1024 * 1024
        ),
    )(tiles, dest, from_left, from_right, edge, proj_left, proj_right)


def from_behind(value, axis, steps):
    count = lax.axis_size(axis)
    pairs = [(source, (source + steps) % count) for source in range(count)]
    return lax.ppermute(value, axis, pairs)


def body(
    corner_left, corner_right, edge_top, proj_left, proj_right, row_order, block_size, block_sector, sector_owner,
):
    from_left = from_behind(corner_left, "col", 1)[0, 0]
    from_right = from_behind(corner_right, "col", -1)[0, 0]
    dest, tiles = plan(
        sector_owner,
        row_order.reshape(100, LANES),
        block_size.reshape(1, LANES),
        block_sector.reshape(1, LANES),
    )
    edge = jnp.transpose(edge_top[0, 0], (1, 0, 2))
    left = jnp.transpose(proj_left[0, 0], (1, 0, 2))
    new_left, new_right, sector_gram = column(tiles, dest, from_left, from_right, edge, left, proj_right[0, 0])
    return (new_left[None, None], new_right[None, None], sector_gram[None, None])


def solution(mesh):
    in_specs = (
        P("col", "row", None, None),
        P("col", "row", None, None),
        P("col", "row", None, "sec", None),
        P("col", "row", None, "sec", None),
        P("col", "row", "sec", None, None),
        P("col", "row", "sec", None),
        P("col", "row", "sec", None),
        P("col", "row", "sec", None, None),
        P(),
    )
    out_specs = (
        P("col", "row", None, None),
        P("col", "row", None, None),
        P("col", ("row", "sec"), None, None),
    )
    return jax.shard_map(body, mesh=mesh, in_specs=in_specs, out_specs=out_specs, check_vma=False)
```

```python
import functools

import jax
import jax.numpy as jnp
from jax import lax
from jax.experimental import pallas as pl
from jax.experimental.pallas import tpu as pltpu
from jax.sharding import PartitionSpec as P

CHI = 256
UNITS = 50
OWNERS = 16
LANES = 128
TILE = 16
TILES = 32
CAP_TILES = 144
EMPTY = TILES - 1
GROUP = 10
STEPS = UNITS // GROUP
HALF = 128
PACKED = 2 * HALF + TILE
Z_CHIPS = 4
EPSILON = 1e-06
MESH = pl.DeviceIdType.MESH

F32 = jnp.float32
BF16 = jnp.bfloat16


def dot(x, y):
    return lax.dot_general(x, y, (((1,), (0,)), ((), ())), preferred_element_type=F32)


def dot_nt(x, y):
    return lax.dot_general(x, y, (((1,), (1,)), ((), ())), preferred_element_type=F32)


def dot_tn(x, y):
    return lax.dot_general(x, y, (((0,), (0,)), ((), ())), preferred_element_type=F32)


def iota(shape, axis):
    return lax.broadcasted_iota(jnp.int32, shape, axis)


def ones_where(mask):
    return jnp.where(mask, 1.0, 0.0).astype(BF16)


def find_owners(owner_ref, order_ref, size_ref, sector_ref):
    sector = sector_ref[...]
    named = jnp.zeros((1, LANES), F32)
    for s in range(OWNERS):
        named = jnp.where(sector == s, (owner_ref[s] + 1).astype(F32), named)
    up = iota((LANES, LANES), 0)
    across = iota((LANES, LANES), 1)
    steps = ones_where(up == across) - ones_where(up + 1 == across)
    sizes = jnp.broadcast_to(size_ref[...].astype(F32), (TILE, LANES)).astype(BF16)
    starts = dot(sizes, ones_where(up < across))[0:1]
    delta = dot(jnp.broadcast_to(named, (TILE, LANES)).astype(BF16), steps)[0:1]
    start_hi = jnp.floor((starts + 0.5) * (1.0 / LANES))
    start_lo = starts - LANES * start_hi
    place_hi = iota((112, LANES), 0).astype(F32)
    impulses = dot_nt(
        jnp.where(place_hi == start_hi, delta, 0.0).astype(BF16),
        ones_where(up.astype(F32) == start_lo),
    ).astype(BF16)
    inside = dot(impulses, ones_where(up <= across))
    totals = jnp.broadcast_to(inside[:, LANES - 1:LANES], (112, LANES)).astype(BF16)
    listed = inside + dot(ones_where(iota((112, 112), 1) < iota((112, 112), 0)), totals)
    bonds = (iota((CHI // TILE, TILE, LANES), 0) * TILE + iota((CHI // TILE, TILE, LANES), 1)).astype(F32).astype(BF16)
    units = (iota((4, TILE, LANES), 0) * TILE + iota((4, TILE, LANES), 1)).astype(F32).astype(BF16)
    one, zero = jnp.ones((), BF16), jnp.zeros((), BF16)
    owned = jnp.zeros((64, CHI), F32)
    for first in range(0, 100, 20):
        left, right = [], []
        for h in range(first, first + 20):
            order = order_ref[:, h * LANES:(h + 1) * LANES].astype(F32)
            bond = jnp.floor((order + 0.5) * (1.0 / UNITS))
            unit = order - UNITS * bond
            bond, unit, name = (
                jnp.broadcast_to(x, (TILE, LANES)).astype(BF16)[None] for x in (bond, unit, listed[h:h + 1])
            )
            left.append(jnp.where(units == unit, name, zero).reshape(64, LANES))
            right.append(jnp.where(bonds == bond, one, zero).reshape(CHI, LANES))
        owned = owned + dot_nt(jnp.concatenate(left, axis=1), jnp.concatenate(right, axis=1))
    return owned


def plan(owner_ref, order_ref, size_ref, sector_ref, dest_ref, tile_ref):
    owned = find_owners(owner_ref, order_ref, size_ref, sector_ref)
    hits = [owned == float(o + 1) for o in range(OWNERS)]
    onehot = [ones_where(hit) for hit in hits]
    ranks = dot(jnp.concatenate(onehot, axis=0), ones_where(iota((CHI, CHI), 0) <= iota((CHI, CHI), 1)))
    offset = jnp.zeros((64, 1), F32)
    dest = jnp.full((64, CHI), -1.0, F32)
    lane = iota((64, LANES), 1)
    tile_counts = jnp.zeros((64, LANES), F32)
    tile_offsets = jnp.zeros((64, LANES), F32)
    for o in range(OWNERS):
        rank = ranks[o * 64:(o + 1) * 64]
        tiles = jnp.floor((rank[:, CHI - 1:CHI] + (TILE - 1)) * (1.0 / TILE))
        dest = jnp.where(hits[o], (TILE * offset - 1.0) + rank, dest)
        tile_counts = jnp.where(lane == o, tiles, tile_counts)
        tile_offsets = jnp.where(lane == o, offset, tile_offsets)
        offset = offset + tiles
    dest_ref[...] = dest
    eye = ones_where(iota((OWNERS, LANES), 0) == iota((OWNERS, LANES), 1))
    counts = dot_nt(eye, tile_counts.astype(BF16))
    offsets = dot_nt(eye, tile_offsets.astype(BF16))
    sofar = dot(counts.astype(BF16), ones_where(iota((64, 64), 0) < iota((64, 64), 1)))
    chunk = iota((OWNERS, 64), 1)
    base = offsets - sofar + (chunk * TILES).astype(F32)
    previous = jnp.where(chunk == 0, 0.0, pltpu.roll(base, 1, 1))
    jump = base - previous
    place = iota((OWNERS, CHI), 1).astype(F32)
    tile = place
    for u in range(UNITS):
        tile = tile + jnp.where(place >= sofar[:, u:u + 1], jump[:, u:u + 1], 0.0)
    used = sofar[:, UNITS - 1:UNITS] + counts[:, UNITS - 1:UNITS]
    tile_ref[...] = jnp.where(place < used, tile, float(EMPTY)).astype(jnp.int32)


def sort_matrix(place):
    place = jnp.broadcast_to(place, (TILE, CHI))
    low = jnp.where(place < CHI, place, -1.0).astype(BF16)
    high = jnp.where(place >= CHI, place - CHI, -1.0).astype(BF16)
    rows = iota((CHI // TILE, TILE, CHI), 0) * TILE + iota((CHI // TILE, TILE, CHI), 1)
    rows = rows.astype(F32).astype(BF16)
    one, zero = jnp.ones((), BF16), jnp.zeros((), BF16)
    return jnp.concatenate(
        [jnp.where(rows == part[None], one, zero).reshape(CHI, CHI) for part in (low, high)], axis=0
    )


def pack(gram):
    upper, corner, lower = gram[:HALF, :HALF], gram[:HALF, HALF:], gram[HALF:, HALF:]
    row, col = iota((HALF, HALF), 0), iota((HALF, HALF), 1)
    diagonal = jnp.sum(jnp.where(row == col, lower, 0.0), axis=0, keepdims=True)
    return jnp.concatenate(
        [jnp.where(row <= col, upper, lower), corner, jnp.broadcast_to(diagonal, (TILE, HALF))], axis=0
    )


def unpack(packed):
    square, corner, diagonal = packed[:HALF], packed[HALF:CHI], packed[CHI:CHI + 1]
    row, col = iota((HALF, HALF), 0), iota((HALF, HALF), 1)
    turned = square.T
    upper = jnp.where(row <= col, square, turned)
    lower = jnp.where(row == col, diagonal, jnp.where(row > col, square, turned))
    return jnp.concatenate(
        [jnp.concatenate([upper, corner], axis=1), jnp.concatenate([corner.T, lower], axis=1)], axis=0
    )


def normalized(total):
    mean = jnp.sum(total * total, keepdims=True) * (1.0 / (CHI * CHI))
    return total * lax.rsqrt(mean + EPSILON)


def column_kernel(
    owner_ref, order_hbm, size_hbm, sector_hbm, left_hbm, right_hbm, edge_hbm, proj_left_hbm, proj_right_hbm,
    out_left, out_right, out_gram,
    order, sizes, sectors, dest, tile_plan, tile_list, from_left, from_right,
    edge, proj_left, proj_right, enlarged, wide, sorted_rows, listed,
    left_sum, right_sum, left_other, right_other,
    gram_sum, mine, to_mate, from_mate, to_row, from_row, to_sec, from_sec,
    list_sem, tile_sem, shift_send, shift_recv, load_sem, corner_send, corner_recv, mate_send, mate_recv, row_send, row_recv, sec_send, sec_recv, result_sem,
):
    col, row, sec = lax.axis_index("col"), lax.axis_index("row"), lax.axis_index("sec")
    z, core = row // 2, row % 2
    mate = {"row": z * 2 + (1 - core)}
    partner = {"sec": 1 - sec}
    ahead = [{"row": ((z + dz) % Z_CHIPS) * 2 + core} for dz in range(1, Z_CHIPS)]

    sides = [{"col": (col + 1) % 8}, {"col": (col + 7) % 8}]
    others = [mate, partner] + ahead + sides

    barrier = pltpu.get_barrier_semaphore()
    for other in others:
        pl.semaphore_signal(barrier, inc=1, device_id=other, device_id_type=MESH)

    pairs = ((edge_hbm, edge), (proj_left_hbm, proj_left), (proj_right_hbm, proj_right))

    def load(k, i):
        part = pl.ds(i * GROUP, GROUP)
        return pltpu.make_async_copy(pairs[k][0].at[part], pairs[k][1].at[part], load_sem.at[k, i])

    lists = [
        pltpu.make_async_copy(source, target, list_sem.at[k])
        for k, (source, target) in enumerate(((order_hbm, order), (size_hbm, sizes), (sector_hbm, sectors)))
    ]
    for copy in lists:
        copy.start()
    for i in range(STEPS):
        load(0, i).start()
        load(1, i).start()
    for i in range(STEPS):
        load(2, i).start()

    pl.semaphore_wait(barrier, len(others))
    shifts = [
        pltpu.make_async_remote_copy(
            src_ref=source, dst_ref=target, send_sem=shift_send.at[k], recv_sem=shift_recv.at[k],
            device_id=sides[k], device_id_type=MESH,
        )
        for k, (source, target) in enumerate(((left_hbm, from_left), (right_hbm, from_right)))
    ]
    for copy in shifts:
        copy.start()
    for copy in lists:
        copy.wait()
    plan(owner_ref, order, sizes, sectors, dest, tile_plan)
    tile_copy = pltpu.make_async_copy(tile_plan, tile_list, tile_sem)
    tile_copy.start()
    shifts[0].wait()

    left_sum[...] = jnp.zeros_like(left_sum)
    right_sum[...] = jnp.zeros_like(right_sum)

    @pl.loop(0, STEPS)
    def _(i):
        load(0, i).wait()
        load(1, i).wait()
        for j in range(GROUP):
            enlarged[pl.ds(j * CHI, CHI), :] = dot(from_left[...], edge[i * GROUP + j]).astype(BF16)
        chunk = proj_left[pl.ds(i * GROUP, GROUP)].reshape(GROUP * CHI, CHI)
        left_sum[...] += dot_tn(chunk, enlarged[...])
        for j in range(GROUP):
            u = i * GROUP + j
            ordered = dot(sort_matrix(dest[pl.ds(u, 1), :]), enlarged[pl.ds(j * CHI, CHI), :])
            sorted_rows[pl.ds(u * TILES, TILES)] = ordered.astype(BF16).reshape(TILES, TILE, CHI)

    def corner_copy(k):
        source, target = ((left_sum, left_other), (right_sum, right_other))[k]
        return pltpu.make_async_remote_copy(
            src_ref=source, dst_ref=target, send_sem=corner_send.at[k], recv_sem=corner_recv.at[k],
            device_id=partner, device_id_type=MESH,
        )

    corner_copy(0).start()
    shifts[1].wait()

    @pl.loop(0, STEPS)
    def _(i):
        load(2, i).wait()
        for j in range(GROUP):
            wide[:, pl.ds(j * CHI, CHI)] = dot(edge[i * GROUP + j], from_right[...]).astype(BF16)
        chunk = proj_right[pl.ds(i * GROUP, GROUP)].reshape(GROUP * CHI, CHI)
        right_sum[...] += dot(wide[...], chunk)

    corner_copy(1).start()
    tile_copy.wait()

    def result(k):
        source, target = ((left_sum, out_left), (right_sum, out_right), (gram_sum, out_gram))[k]
        return pltpu.make_async_copy(source, target, result_sem.at[k])

    def owner_gram(k, owner):
        for t in range(CAP_TILES):
            tile = jnp.minimum(jnp.maximum(tile_list[owner, t], 0), UNITS * TILES - 1)
            listed[k, pl.ds(t * TILE, TILE), :] = sorted_rows[tile]
        rows = listed[k]
        return pack(dot_tn(rows, rows))

    def mate_copy(i):
        return pltpu.make_async_remote_copy(
            src_ref=to_mate.at[i], dst_ref=from_mate.at[i], send_sem=mate_send.at[i], recv_sem=mate_recv.at[i],
            device_id=mate, device_id_type=MESH,
        )

    def row_copy(j):
        target = {"row": ((z + 1 + j // 2) % Z_CHIPS) * 2 + core}
        return pltpu.make_async_remote_copy(
            src_ref=to_row.at[j], dst_ref=from_row.at[j], send_sem=row_send.at[j], recv_sem=row_recv.at[j],
            device_id=target, device_id_type=MESH,
        )

    sec_copy = pltpu.make_async_remote_copy(
        src_ref=to_sec, dst_ref=from_sec, send_sem=sec_send, recv_sem=sec_recv,
        device_id=partner, device_id_type=MESH,
    )

    @pl.loop(0, 2 * Z_CHIPS)
    def _(i):
        z_owner = (z + 1 + i // 2) % Z_CHIPS
        sec_owner = (sec + 1 + i) % 2
        to_mate[i] = owner_gram(0, z_owner * 4 + (1 - core) * 2 + sec_owner)
        mate_copy(i).start()
        mine[i] = owner_gram(1, z_owner * 4 + core * 2 + sec_owner)

        @pl.when((i >= 1) & (i <= 6))
        def _():
            mate_copy(i - 1).wait_recv()
            to_row[i - 1] = (mine[i - 1] + from_mate[i - 1]).astype(BF16)
            row_copy(i - 1).start()

    def column_sum(r):
        mate_copy(6 + r).wait_recv()
        total = mine[6 + r] + from_mate[6 + r]
        for k in range(Z_CHIPS - 1):
            row_copy(2 * k + r).wait_recv()
            total = total + from_row[2 * k + r].astype(F32)
        return total

    to_sec[...] = column_sum(0).astype(BF16)
    sec_copy.start()
    corner_copy(0).wait()
    left_sum[...] = normalized(left_sum[...] + left_other[...])
    result(0).start()
    corner_copy(1).wait()
    right_sum[...] = normalized(right_sum[...] + right_other[...])
    result(1).start()
    total = column_sum(1)
    sec_copy.wait_recv()
    gram_sum[...] = unpack(total + from_sec[...].astype(F32))
    result(2).start()
    for i in range(2 * Z_CHIPS):
        mate_copy(i).wait_send()
    for j in range(2 * (Z_CHIPS - 1)):
        row_copy(j).wait_send()
    sec_copy.wait_send()
    for k in range(3):
        result(k).wait()


def column(sector_owner, row_order, block_size, block_sector, corner_left, corner_right, edge, proj_left, proj_right):
    hbm = pl.BlockSpec(memory_space=pltpu.HBM)
    square = jax.ShapeDtypeStruct((CHI, CHI), F32)
    whole = pltpu.VMEM((UNITS, CHI, CHI), BF16)
    dma = pltpu.SemaphoreType.DMA
    return pl.pallas_call(
        column_kernel,
        in_specs=[pl.BlockSpec(memory_space=pltpu.SMEM)] + [hbm] * 8,
        out_specs=(hbm, hbm, hbm),
        out_shape=(square, square, square),
        scratch_shapes=[
            pltpu.VMEM((1, UNITS * CHI), jnp.int32),
            pltpu.VMEM((1, LANES), jnp.int32),
            pltpu.VMEM((1, LANES), jnp.int32),
            pltpu.VMEM((64, CHI), F32),
            pltpu.VMEM((OWNERS, CHI), jnp.int32),
            pltpu.SMEM((OWNERS, CHI), jnp.int32),
            pltpu.VMEM((CHI, CHI), BF16),
            pltpu.VMEM((CHI, CHI), BF16),
            whole, whole, whole,
            pltpu.VMEM((GROUP * CHI, CHI), BF16),
            pltpu.VMEM((CHI, GROUP * CHI), BF16),
            pltpu.VMEM((UNITS * TILES, TILE, CHI), BF16),
            pltpu.VMEM((2, CAP_TILES * TILE, CHI), BF16),
            pltpu.VMEM((CHI, CHI), F32), pltpu.VMEM((CHI, CHI), F32),
            pltpu.VMEM((CHI, CHI), F32), pltpu.VMEM((CHI, CHI), F32),
            pltpu.VMEM((CHI, CHI), F32),
            pltpu.VMEM((8, PACKED, HALF), F32),
            pltpu.VMEM((8, PACKED, HALF), F32),
            pltpu.VMEM((8, PACKED, HALF), F32),
            pltpu.VMEM((6, PACKED, HALF), BF16),
            pltpu.VMEM((6, PACKED, HALF), BF16),
            pltpu.VMEM((PACKED, HALF), BF16),
            pltpu.VMEM((PACKED, HALF), BF16),
            dma((3,)), dma, dma((2,)), dma((2,)),
            dma((3, STEPS)), dma((2,)), dma((2,)), dma((8,)), dma((8,)), dma((6,)), dma((6,)), dma, dma, dma((3,)),
        ],
        cost_estimate=pl.CostEstimate(flops=9 * 2 * 12800 * 65536, bytes_accessed=24 << 20, transcendentals=0),
        compiler_params=pltpu.CompilerParams(
            collective_id=0, has_side_effects=True, vmem_limit_bytes=58 * 1024 * 1024
        ),
    )(sector_owner, row_order, block_size, block_sector, corner_left, corner_right, edge, proj_left, proj_right)


def finish_kernel(*refs):
    copies = [pltpu.make_async_copy(refs[k], refs[3 + k], refs[6].at[k]) for k in range(3)]
    for copy in copies:
        copy.start()
    for copy in copies:
        copy.wait()


def finish(*results):
    hbm = pl.BlockSpec(memory_space=pltpu.HBM)
    square = jax.ShapeDtypeStruct((CHI, CHI), F32)
    return pl.pallas_call(
        finish_kernel,
        in_specs=[hbm] * 3,
        out_specs=(hbm,) * 3,
        out_shape=(square,) * 3,
        scratch_shapes=[pltpu.SemaphoreType.DMA((3,))],
        compiler_params=pltpu.CompilerParams(vmem_limit_bytes=60 * 1024 * 1024),
    )(*results)


def body(
    corner_left, corner_right, edge_top, proj_left, proj_right, row_order, block_size, block_sector, sector_owner,
):
    sums = column(
        sector_owner,
        row_order.reshape(1, UNITS * CHI),
        block_size.reshape(1, LANES),
        block_sector.reshape(1, LANES),
        corner_left[0, 0],
        corner_right[0, 0],
        jnp.transpose(edge_top[0, 0], (1, 0, 2)),
        jnp.transpose(proj_left[0, 0], (1, 0, 2)),
        proj_right[0, 0],
    )
    return tuple(out[None, None] for out in finish(*sums))


def solution(mesh):
    in_specs = (
        P("col", "row", None, None),
        P("col", "row", None, None),
        P("col", "row", None, "sec", None),
        P("col", "row", None, "sec", None),
        P("col", "row", "sec", None, None),
        P("col", "row", "sec", None),
        P("col", "row", "sec", None),
        P("col", "row", "sec", None, None),
        P(),
    )
    out_specs = (
        P("col", "row", None, None),
        P("col", "row", None, None),
        P("col", ("row", "sec"), None, None),
    )
    return jax.shard_map(body, mesh=mesh, in_specs=in_specs, out_specs=out_specs, check_vma=False)
```

```python
import functools

import jax
import jax.numpy as jnp
from jax import lax
from jax.experimental import pallas as pl
from jax.experimental.pallas import tpu as pltpu
from jax.sharding import PartitionSpec as P

CHI = 256
UNITS = 50
OWNERS = 16
LANES = 128
TILE = 16
TILES = 32
CAP_TILES = 144
EMPTY = TILES - 1
GROUP = 10
STEPS = UNITS // GROUP
HALF = 128
PACKED = 2 * HALF + TILE
Z_CHIPS = 4
EPSILON = 1e-06
MESH = pl.DeviceIdType.MESH

F32 = jnp.float32
BF16 = jnp.bfloat16


def dot(x, y):
    return lax.dot_general(x, y, (((1,), (0,)), ((), ())), preferred_element_type=F32)


def dot_nt(x, y):
    return lax.dot_general(x, y, (((1,), (1,)), ((), ())), preferred_element_type=F32)


def dot_tn(x, y):
    return lax.dot_general(x, y, (((0,), (0,)), ((), ())), preferred_element_type=F32)


def iota(shape, axis):
    return lax.broadcasted_iota(jnp.int32, shape, axis)


def ones_where(mask):
    return jnp.where(mask, 1.0, 0.0).astype(BF16)


def find_owners(owner_ref, order_ref, size_ref, sector_ref):
    sector = sector_ref[...]
    named = jnp.zeros((1, LANES), F32)
    for s in range(OWNERS):
        named = jnp.where(sector == s, (owner_ref[s] + 1).astype(F32), named)
    up = iota((LANES, LANES), 0)
    across = iota((LANES, LANES), 1)
    steps = ones_where(up == across) - ones_where(up + 1 == across)
    sizes = jnp.broadcast_to(size_ref[...].astype(F32), (TILE, LANES)).astype(BF16)
    starts = dot(sizes, ones_where(up < across))[0:1]
    delta = dot(jnp.broadcast_to(named, (TILE, LANES)).astype(BF16), steps)[0:1]
    start_hi = jnp.floor((starts + 0.5) * (1.0 / LANES))
    start_lo = starts - LANES * start_hi
    place_hi = iota((112, LANES), 0).astype(F32)
    impulses = dot_nt(
        jnp.where(place_hi == start_hi, delta, 0.0).astype(BF16),
        ones_where(up.astype(F32) == start_lo),
    ).astype(BF16)
    inside = dot(impulses, ones_where(up <= across))
    totals = jnp.broadcast_to(inside[:, LANES - 1:LANES], (112, LANES)).astype(BF16)
    listed = inside + dot(ones_where(iota((112, 112), 1) < iota((112, 112), 0)), totals)
    bonds = (iota((CHI // TILE, TILE, LANES), 0) * TILE + iota((CHI // TILE, TILE, LANES), 1)).astype(F32).astype(BF16)
    units = (iota((4, TILE, LANES), 0) * TILE + iota((4, TILE, LANES), 1)).astype(F32).astype(BF16)
    one, zero = jnp.ones((), BF16), jnp.zeros((), BF16)
    owned = jnp.zeros((64, CHI), F32)
    for first in range(0, 100, 20):
        left, right = [], []
        for h in range(first, first + 20):
            order = order_ref[:, h * LANES:(h + 1) * LANES].astype(F32)
            bond = jnp.floor((order + 0.5) * (1.0 / UNITS))
            unit = order - UNITS * bond
            bond, unit, name = (
                jnp.broadcast_to(x, (TILE, LANES)).astype(BF16)[None] for x in (bond, unit, listed[h:h + 1])
            )
            left.append(jnp.where(units == unit, name, zero).reshape(64, LANES))
            right.append(jnp.where(bonds == bond, one, zero).reshape(CHI, LANES))
        owned = owned + dot_nt(jnp.concatenate(left, axis=1), jnp.concatenate(right, axis=1))
    return owned


def plan(owner_ref, order_ref, size_ref, sector_ref, dest_ref, tile_ref):
    owned = find_owners(owner_ref, order_ref, size_ref, sector_ref)
    hits = [owned == float(o + 1) for o in range(OWNERS)]
    onehot = [ones_where(hit) for hit in hits]
    ranks = dot(jnp.concatenate(onehot, axis=0), ones_where(iota((CHI, CHI), 0) <= iota((CHI, CHI), 1)))
    offset = jnp.zeros((64, 1), F32)
    dest = jnp.full((64, CHI), -1.0, F32)
    lane = iota((64, LANES), 1)
    tile_counts = jnp.zeros((64, LANES), F32)
    tile_offsets = jnp.zeros((64, LANES), F32)
    for o in range(OWNERS):
        rank = ranks[o * 64:(o + 1) * 64]
        tiles = jnp.floor((rank[:, CHI - 1:CHI] + (TILE - 1)) * (1.0 / TILE))
        dest = jnp.where(hits[o], (TILE * offset - 1.0) + rank, dest)
        tile_counts = jnp.where(lane == o, tiles, tile_counts)
        tile_offsets = jnp.where(lane == o, offset, tile_offsets)
        offset = offset + tiles
    dest_ref[...] = dest
    eye = ones_where(iota((OWNERS, LANES), 0) == iota((OWNERS, LANES), 1))
    counts = dot_nt(eye, tile_counts.astype(BF16))
    offsets = dot_nt(eye, tile_offsets.astype(BF16))
    sofar = dot(counts.astype(BF16), ones_where(iota((64, 64), 0) < iota((64, 64), 1)))
    chunk = iota((OWNERS, 64), 1)
    base = offsets - sofar + (chunk * TILES).astype(F32)
    previous = jnp.where(chunk == 0, 0.0, pltpu.roll(base, 1, 1))
    jump = base - previous
    place = iota((OWNERS, CHI), 1).astype(F32)
    tile = place
    for u in range(UNITS):
        tile = tile + jnp.where(place >= sofar[:, u:u + 1], jump[:, u:u + 1], 0.0)
    used = sofar[:, UNITS - 1:UNITS] + counts[:, UNITS - 1:UNITS]
    tile_ref[...] = jnp.where(place < used, tile, float(EMPTY)).astype(jnp.int32)


def sort_matrix(place):
    place = jnp.broadcast_to(place, (TILE, CHI))
    low = jnp.where(place < CHI, place, -1.0).astype(BF16)
    high = jnp.where(place >= CHI, place - CHI, -1.0).astype(BF16)
    rows = iota((CHI // TILE, TILE, CHI), 0) * TILE + iota((CHI // TILE, TILE, CHI), 1)
    rows = rows.astype(F32).astype(BF16)
    one, zero = jnp.ones((), BF16), jnp.zeros((), BF16)
    return jnp.concatenate(
        [jnp.where(rows == part[None], one, zero).reshape(CHI, CHI) for part in (low, high)], axis=0
    )


def pack(gram):
    upper, corner, lower = gram[:HALF, :HALF], gram[:HALF, HALF:], gram[HALF:, HALF:]
    row, col = iota((HALF, HALF), 0), iota((HALF, HALF), 1)
    diagonal = jnp.sum(jnp.where(row == col, lower, 0.0), axis=0, keepdims=True)
    return jnp.concatenate(
        [jnp.where(row <= col, upper, lower), corner, jnp.broadcast_to(diagonal, (TILE, HALF))], axis=0
    )


def unpack(packed):
    square, corner, diagonal = packed[:HALF], packed[HALF:CHI], packed[CHI:CHI + 1]
    row, col = iota((HALF, HALF), 0), iota((HALF, HALF), 1)
    turned = square.T
    upper = jnp.where(row <= col, square, turned)
    lower = jnp.where(row == col, diagonal, jnp.where(row > col, square, turned))
    return jnp.concatenate(
        [jnp.concatenate([upper, corner], axis=1), jnp.concatenate([corner.T, lower], axis=1)], axis=0
    )


def normalized(total):
    mean = jnp.sum(total * total, keepdims=True) * (1.0 / (CHI * CHI))
    return total * lax.rsqrt(mean + EPSILON)


def column_kernel(
    owner_ref, order_hbm, size_hbm, sector_hbm, left_hbm, right_hbm, edge_hbm, proj_left_hbm, proj_right_hbm,
    out_left, out_right, out_gram,
    order, sizes, sectors, dest, tile_plan, tile_list, from_left, from_right,
    edge, proj_left, proj_right, enlarged, wide, sorted_rows, listed,
    left_sum, right_sum, left_other, right_other,
    gram_sum, mine, to_mate, from_mate, to_row, from_row, to_sec, from_sec,
    list_sem, tile_sem, shift_send, shift_recv, load_sem, corner_send, corner_recv, mate_send, mate_recv, row_send, row_recv, sec_send, sec_recv, result_sem,
):
    col, row, sec = lax.axis_index("col"), lax.axis_index("row"), lax.axis_index("sec")
    z, core = row // 2, row % 2
    mate = {"row": z * 2 + (1 - core)}
    partner = {"sec": 1 - sec}
    ahead = [{"row": ((z + dz) % Z_CHIPS) * 2 + core} for dz in range(1, Z_CHIPS)]

    sides = [{"col": (col + 1) % 8}, {"col": (col + 7) % 8}]
    others = [mate, partner] + ahead + sides

    barrier = pltpu.get_barrier_semaphore()
    for other in others:
        pl.semaphore_signal(barrier, inc=1, device_id=other, device_id_type=MESH)

    pairs = ((edge_hbm, edge), (proj_left_hbm, proj_left), (proj_right_hbm, proj_right))

    def load(k, i):
        part = pl.ds(i * GROUP, GROUP)
        return pltpu.make_async_copy(pairs[k][0].at[part], pairs[k][1].at[part], load_sem.at[k, i])

    lists = [
        pltpu.make_async_copy(source, target, list_sem.at[k])
        for k, (source, target) in enumerate(((order_hbm, order), (size_hbm, sizes), (sector_hbm, sectors)))
    ]
    for copy in lists:
        copy.start()
    for i in range(STEPS):
        load(0, i).start()
        load(1, i).start()
    for i in range(STEPS):
        load(2, i).start()

    pl.semaphore_wait(barrier, len(others))
    shifts = [
        pltpu.make_async_remote_copy(
            src_ref=source, dst_ref=target, send_sem=shift_send.at[k], recv_sem=shift_recv.at[k],
            device_id=sides[k], device_id_type=MESH,
        )
        for k, (source, target) in enumerate(((left_hbm, from_left), (right_hbm, from_right)))
    ]
    for copy in shifts:
        copy.start()
    for copy in lists:
        copy.wait()
    plan(owner_ref, order, sizes, sectors, dest, tile_plan)
    tile_copy = pltpu.make_async_copy(tile_plan, tile_list, tile_sem)
    tile_copy.start()
    shifts[0].wait()

    left_sum[...] = jnp.zeros_like(left_sum)
    right_sum[...] = jnp.zeros_like(right_sum)

    @pl.loop(0, STEPS)
    def _(i):
        load(0, i).wait()
        load(1, i).wait()
        for j in range(GROUP):
            enlarged[pl.ds(j * CHI, CHI), :] = dot(from_left[...], edge[i * GROUP + j]).astype(BF16)
        chunk = proj_left[pl.ds(i * GROUP, GROUP)].reshape(GROUP * CHI, CHI)
        left_sum[...] += dot_tn(chunk, enlarged[...])
        for j in range(GROUP):
            u = i * GROUP + j
            ordered = dot(sort_matrix(dest[pl.ds(u, 1), :]), enlarged[pl.ds(j * CHI, CHI), :])
            sorted_rows[pl.ds(u * TILES, TILES)] = ordered.astype(BF16).reshape(TILES, TILE, CHI)

    def corner_copy(k):
        source, target = ((left_sum, left_other), (right_sum, right_other))[k]
        return pltpu.make_async_remote_copy(
            src_ref=source, dst_ref=target, send_sem=corner_send.at[k], recv_sem=corner_recv.at[k],
            device_id=partner, device_id_type=MESH,
        )

    corner_copy(0).start()
    shifts[1].wait()

    @pl.loop(0, STEPS)
    def _(i):
        load(2, i).wait()
        for j in range(GROUP):
            wide[:, pl.ds(j * CHI, CHI)] = dot(edge[i * GROUP + j], from_right[...]).astype(BF16)
        chunk = proj_right[pl.ds(i * GROUP, GROUP)].reshape(GROUP * CHI, CHI)
        right_sum[...] += dot(wide[...], chunk)

    corner_copy(1).start()
    tile_copy.wait()

    def result(k):
        source, target = ((left_sum, out_left), (right_sum, out_right), (gram_sum, out_gram))[k]
        return pltpu.make_async_copy(source, target, result_sem.at[k])

    def owner_gram(k, owner):
        for t in range(CAP_TILES):
            tile = jnp.minimum(jnp.maximum(tile_list[owner, t], 0), UNITS * TILES - 1)
            listed[k, pl.ds(t * TILE, TILE), :] = sorted_rows[tile]
        rows = listed[k]
        return pack(dot_tn(rows, rows))

    def mate_copy(i):
        return pltpu.make_async_remote_copy(
            src_ref=to_mate.at[i], dst_ref=from_mate.at[i], send_sem=mate_send.at[i], recv_sem=mate_recv.at[i],
            device_id=mate, device_id_type=MESH,
        )

    def row_copy(j):
        target = {"row": ((z + 1 + j // 2) % Z_CHIPS) * 2 + core}
        return pltpu.make_async_remote_copy(
            src_ref=to_row.at[j], dst_ref=from_row.at[j], send_sem=row_send.at[j], recv_sem=row_recv.at[j],
            device_id=target, device_id_type=MESH,
        )

    sec_copy = pltpu.make_async_remote_copy(
        src_ref=to_sec, dst_ref=from_sec, send_sem=sec_send, recv_sem=sec_recv,
        device_id=partner, device_id_type=MESH,
    )

    @pl.loop(0, 2 * Z_CHIPS)
    def _(i):
        z_owner = (z + 1 + i // 2) % Z_CHIPS
        sec_owner = (sec + 1 + i) % 2
        to_mate[i] = owner_gram(0, z_owner * 4 + (1 - core) * 2 + sec_owner)
        mate_copy(i).start()
        mine[i] = owner_gram(1, z_owner * 4 + core * 2 + sec_owner)

        @pl.when((i >= 1) & (i <= 6))
        def _():
            mate_copy(i - 1).wait_recv()
            to_row[i - 1] = (mine[i - 1] + from_mate[i - 1]).astype(BF16)
            row_copy(i - 1).start()

    def column_sum(r):
        mate_copy(6 + r).wait_recv()
        total = mine[6 + r] + from_mate[6 + r]
        for k in range(Z_CHIPS - 1):
            row_copy(2 * k + r).wait_recv()
            total = total + from_row[2 * k + r].astype(F32)
        return total

    to_sec[...] = column_sum(0).astype(BF16)
    sec_copy.start()
    corner_copy(0).wait()
    left_sum[...] = normalized(left_sum[...] + left_other[...])
    result(0).start()
    corner_copy(1).wait()
    right_sum[...] = normalized(right_sum[...] + right_other[...])
    result(1).start()
    total = column_sum(1)
    sec_copy.wait_recv()
    gram_sum[...] = unpack(total + from_sec[...].astype(F32))
    result(2).start()
    for i in range(2 * Z_CHIPS):
        mate_copy(i).wait_send()
    for j in range(2 * (Z_CHIPS - 1)):
        row_copy(j).wait_send()
    sec_copy.wait_send()
    for k in range(3):
        result(k).wait()


def column(sector_owner, row_order, block_size, block_sector, corner_left, corner_right, edge, proj_left, proj_right):
    hbm = pl.BlockSpec(memory_space=pltpu.HBM)
    square = jax.ShapeDtypeStruct((CHI, CHI), F32)
    whole = pltpu.VMEM((UNITS, CHI, CHI), BF16)
    dma = pltpu.SemaphoreType.DMA
    return pl.pallas_call(
        column_kernel,
        in_specs=[pl.BlockSpec(memory_space=pltpu.SMEM)] + [hbm] * 8,
        out_specs=(hbm, hbm, hbm),
        out_shape=(square, square, square),
        scratch_shapes=[
            pltpu.VMEM((1, UNITS * CHI), jnp.int32),
            pltpu.VMEM((1, LANES), jnp.int32),
            pltpu.VMEM((1, LANES), jnp.int32),
            pltpu.VMEM((64, CHI), F32),
            pltpu.VMEM((OWNERS, CHI), jnp.int32),
            pltpu.SMEM((OWNERS, CHI), jnp.int32),
            pltpu.VMEM((CHI, CHI), BF16),
            pltpu.VMEM((CHI, CHI), BF16),
            whole, whole, whole,
            pltpu.VMEM((GROUP * CHI, CHI), BF16),
            pltpu.VMEM((CHI, GROUP * CHI), BF16),
            pltpu.VMEM((UNITS * TILES, TILE, CHI), BF16),
            pltpu.VMEM((2, CAP_TILES * TILE, CHI), BF16),
            pltpu.VMEM((CHI, CHI), F32), pltpu.VMEM((CHI, CHI), F32),
            pltpu.VMEM((CHI, CHI), F32), pltpu.VMEM((CHI, CHI), F32),
            pltpu.VMEM((CHI, CHI), F32),
            pltpu.VMEM((8, PACKED, HALF), F32),
            pltpu.VMEM((8, PACKED, HALF), F32),
            pltpu.VMEM((8, PACKED, HALF), F32),
            pltpu.VMEM((6, PACKED, HALF), BF16),
            pltpu.VMEM((6, PACKED, HALF), BF16),
            pltpu.VMEM((PACKED, HALF), BF16),
            pltpu.VMEM((PACKED, HALF), BF16),
            dma((3,)), dma, dma((2,)), dma((2,)),
            dma((3, STEPS)), dma((2,)), dma((2,)), dma((8,)), dma((8,)), dma((6,)), dma((6,)), dma, dma, dma((3,)),
        ],
        cost_estimate=pl.CostEstimate(flops=9 * 2 * 12800 * 65536, bytes_accessed=24 << 20, transcendentals=0),
        compiler_params=pltpu.CompilerParams(
            collective_id=0, has_side_effects=True, vmem_limit_bytes=58 * 1024 * 1024
        ),
    )(sector_owner, row_order, block_size, block_sector, corner_left, corner_right, edge, proj_left, proj_right)


def finish_kernel(*refs):
    held, load_sem, store_sem = refs[6:]
    loads = [pltpu.make_async_copy(refs[k], held.at[k], load_sem.at[k]) for k in range(3)]
    stores = [pltpu.make_async_copy(held.at[k], refs[3 + k], store_sem.at[k]) for k in range(3)]
    for copy in loads:
        copy.start()
    for k in range(3):
        loads[k].wait()
        stores[k].start()
    for copy in stores:
        copy.wait()


def finish(*results):
    hbm = pl.BlockSpec(memory_space=pltpu.HBM)
    square = jax.ShapeDtypeStruct((CHI, CHI), F32)
    return pl.pallas_call(
        finish_kernel,
        in_specs=[hbm] * 3,
        out_specs=(hbm,) * 3,
        out_shape=(square,) * 3,
        scratch_shapes=[
            pltpu.VMEM((3, CHI, CHI), F32), pltpu.SemaphoreType.DMA((3,)), pltpu.SemaphoreType.DMA((3,)),
        ],
        compiler_params=pltpu.CompilerParams(vmem_limit_bytes=60 * 1024 * 1024),
    )(*results)


def body(
    corner_left, corner_right, edge_top, proj_left, proj_right, row_order, block_size, block_sector, sector_owner,
):
    sums = column(
        sector_owner,
        row_order.reshape(1, UNITS * CHI),
        block_size.reshape(1, LANES),
        block_sector.reshape(1, LANES),
        corner_left[0, 0],
        corner_right[0, 0],
        jnp.transpose(edge_top[0, 0], (1, 0, 2)),
        jnp.transpose(proj_left[0, 0], (1, 0, 2)),
        proj_right[0, 0],
    )
    return tuple(out[None, None] for out in finish(*sums))


def solution(mesh):
    in_specs = (
        P("col", "row", None, None),
        P("col", "row", None, None),
        P("col", "row", None, "sec", None),
        P("col", "row", None, "sec", None),
        P("col", "row", "sec", None, None),
        P("col", "row", "sec", None),
        P("col", "row", "sec", None),
        P("col", "row", "sec", None, None),
        P(),
    )
    out_specs = (
        P("col", "row", None, None),
        P("col", "row", None, None),
        P("col", ("row", "sec"), None, None),
    )
    return jax.shard_map(body, mesh=mesh, in_specs=in_specs, out_specs=out_specs, check_vma=False)
```

```python
import functools

import jax
import jax.numpy as jnp
from jax import lax
from jax.experimental import pallas as pl
from jax.experimental.pallas import tpu as pltpu
from jax.sharding import PartitionSpec as P

CHI = 256
UNITS = 50
OWNERS = 16
LANES = 128
TILE = 16
TILES = 32
CAP_TILES = 144
EMPTY = TILES - 1
GROUP = 10
STEPS = UNITS // GROUP
HALF = 128
PACKED = 2 * HALF + TILE
Z_CHIPS = 4
EPSILON = 1e-06
MESH = pl.DeviceIdType.MESH

F32 = jnp.float32
BF16 = jnp.bfloat16


def dot(x, y):
    return lax.dot_general(x, y, (((1,), (0,)), ((), ())), preferred_element_type=F32)


def dot_nt(x, y):
    return lax.dot_general(x, y, (((1,), (1,)), ((), ())), preferred_element_type=F32)


def dot_tn(x, y):
    return lax.dot_general(x, y, (((0,), (0,)), ((), ())), preferred_element_type=F32)


def iota(shape, axis):
    return lax.broadcasted_iota(jnp.int32, shape, axis)


def ones_where(mask):
    return jnp.where(mask, 1.0, 0.0).astype(BF16)


def find_owners(owner_ref, order_ref, size_ref, sector_ref):
    sector = sector_ref[...]
    named = jnp.zeros((1, LANES), F32)
    for s in range(OWNERS):
        named = jnp.where(sector == s, (owner_ref[s] + 1).astype(F32), named)
    up = iota((LANES, LANES), 0)
    across = iota((LANES, LANES), 1)
    steps = ones_where(up == across) - ones_where(up + 1 == across)
    sizes = jnp.broadcast_to(size_ref[...].astype(F32), (TILE, LANES)).astype(BF16)
    starts = dot(sizes, ones_where(up < across))[0:1]
    delta = dot(jnp.broadcast_to(named, (TILE, LANES)).astype(BF16), steps)[0:1]
    start_hi = jnp.floor((starts + 0.5) * (1.0 / LANES))
    start_lo = starts - LANES * start_hi
    place_hi = iota((112, LANES), 0).astype(F32)
    impulses = dot_nt(
        jnp.where(place_hi == start_hi, delta, 0.0).astype(BF16),
        ones_where(up.astype(F32) == start_lo),
    ).astype(BF16)
    inside = dot(impulses, ones_where(up <= across))
    totals = jnp.broadcast_to(inside[:, LANES - 1:LANES], (112, LANES)).astype(BF16)
    listed = inside + dot(ones_where(iota((112, 112), 1) < iota((112, 112), 0)), totals)
    bonds = (iota((CHI // TILE, TILE, LANES), 0) * TILE + iota((CHI // TILE, TILE, LANES), 1)).astype(F32).astype(BF16)
    units = (iota((4, TILE, LANES), 0) * TILE + iota((4, TILE, LANES), 1)).astype(F32).astype(BF16)
    one, zero = jnp.ones((), BF16), jnp.zeros((), BF16)
    owned = jnp.zeros((64, CHI), F32)
    for first in range(0, 100, 20):
        left, right = [], []
        for h in range(first, first + 20):
            order = order_ref[:, h * LANES:(h + 1) * LANES].astype(F32)
            bond = jnp.floor((order + 0.5) * (1.0 / UNITS))
            unit = order - UNITS * bond
            bond, unit, name = (
                jnp.broadcast_to(x, (TILE, LANES)).astype(BF16)[None] for x in (bond, unit, listed[h:h + 1])
            )
            left.append(jnp.where(units == unit, name, zero).reshape(64, LANES))
            right.append(jnp.where(bonds == bond, one, zero).reshape(CHI, LANES))
        owned = owned + dot_nt(jnp.concatenate(left, axis=1), jnp.concatenate(right, axis=1))
    return owned


def plan(owner_ref, order_ref, size_ref, sector_ref, dest_ref, tile_ref):
    owned = find_owners(owner_ref, order_ref, size_ref, sector_ref)
    hits = [owned == float(o + 1) for o in range(OWNERS)]
    onehot = [ones_where(hit) for hit in hits]
    ranks = dot(jnp.concatenate(onehot, axis=0), ones_where(iota((CHI, CHI), 0) <= iota((CHI, CHI), 1)))
    offset = jnp.zeros((64, 1), F32)
    dest = jnp.full((64, CHI), -1.0, F32)
    lane = iota((64, LANES), 1)
    tile_counts = jnp.zeros((64, LANES), F32)
    tile_offsets = jnp.zeros((64, LANES), F32)
    for o in range(OWNERS):
        rank = ranks[o * 64:(o + 1) * 64]
        tiles = jnp.floor((rank[:, CHI - 1:CHI] + (TILE - 1)) * (1.0 / TILE))
        dest = jnp.where(hits[o], (TILE * offset - 1.0) + rank, dest)
        tile_counts = jnp.where(lane == o, tiles, tile_counts)
        tile_offsets = jnp.where(lane == o, offset, tile_offsets)
        offset = offset + tiles
    dest_ref[...] = dest
    eye = ones_where(iota((OWNERS, LANES), 0) == iota((OWNERS, LANES), 1))
    counts = dot_nt(eye, tile_counts.astype(BF16))
    offsets = dot_nt(eye, tile_offsets.astype(BF16))
    sofar = dot(counts.astype(BF16), ones_where(iota((64, 64), 0) < iota((64, 64), 1)))
    chunk = iota((OWNERS, 64), 1)
    base = offsets - sofar + (chunk * TILES).astype(F32)
    previous = jnp.where(chunk == 0, 0.0, pltpu.roll(base, 1, 1))
    jump = base - previous
    place = iota((OWNERS, CHI), 1).astype(F32)
    tile = place
    for u in range(UNITS):
        tile = tile + jnp.where(place >= sofar[:, u:u + 1], jump[:, u:u + 1], 0.0)
    used = sofar[:, UNITS - 1:UNITS] + counts[:, UNITS - 1:UNITS]
    tile_ref[...] = jnp.where(place < used, tile, float(EMPTY)).astype(jnp.int32)


def sort_matrix(place):
    place = jnp.broadcast_to(place, (TILE, CHI))
    low = jnp.where(place < CHI, place, -1.0).astype(BF16)
    high = jnp.where(place >= CHI, place - CHI, -1.0).astype(BF16)
    rows = iota((CHI // TILE, TILE, CHI), 0) * TILE + iota((CHI // TILE, TILE, CHI), 1)
    rows = rows.astype(F32).astype(BF16)
    one, zero = jnp.ones((), BF16), jnp.zeros((), BF16)
    return jnp.concatenate(
        [jnp.where(rows == part[None], one, zero).reshape(CHI, CHI) for part in (low, high)], axis=0
    )


def pack(gram):
    upper, corner, lower = gram[:HALF, :HALF], gram[:HALF, HALF:], gram[HALF:, HALF:]
    row, col = iota((HALF, HALF), 0), iota((HALF, HALF), 1)
    diagonal = jnp.sum(jnp.where(row == col, lower, 0.0), axis=0, keepdims=True)
    return jnp.concatenate(
        [jnp.where(row <= col, upper, lower), corner, jnp.broadcast_to(diagonal, (TILE, HALF))], axis=0
    )


def unpack(packed):
    square, corner, diagonal = packed[:HALF], packed[HALF:CHI], packed[CHI:CHI + 1]
    row, col = iota((HALF, HALF), 0), iota((HALF, HALF), 1)
    turned = square.T
    upper = jnp.where(row <= col, square, turned)
    lower = jnp.where(row == col, diagonal, jnp.where(row > col, square, turned))
    return jnp.concatenate(
        [jnp.concatenate([upper, corner], axis=1), jnp.concatenate([corner.T, lower], axis=1)], axis=0
    )


def normalized(total):
    mean = jnp.sum(total * total, keepdims=True) * (1.0 / (CHI * CHI))
    return total * lax.rsqrt(mean + EPSILON)


def column_kernel(
    owner_ref, order_hbm, size_hbm, sector_hbm, left_hbm, right_hbm, edge_hbm, proj_left_hbm, proj_right_hbm,
    out_left, out_right, out_gram,
    order, sizes, sectors, dest, tile_plan, tile_list, from_left, from_right,
    edge, proj_left, proj_right, enlarged, wide, sorted_rows, listed_mate, listed_mine,
    left_sum, right_sum, left_other, right_other,
    gram_sum, mine, to_mate, from_mate, to_row, from_row, to_sec, from_sec,
    list_sem, tile_sem, shift_send, shift_recv, load_sem, corner_send, corner_recv, mate_send, mate_recv, row_send, row_recv, sec_send, sec_recv, result_sem,
):
    col, row, sec = lax.axis_index("col"), lax.axis_index("row"), lax.axis_index("sec")
    z, core = row // 2, row % 2
    mate = {"row": z * 2 + (1 - core)}
    partner = {"sec": 1 - sec}
    ahead = [{"row": ((z + dz) % Z_CHIPS) * 2 + core} for dz in range(1, Z_CHIPS)]

    sides = [{"col": (col + 1) % 8}, {"col": (col + 7) % 8}]
    others = [mate, partner] + ahead + sides

    barrier = pltpu.get_barrier_semaphore()
    for other in others:
        pl.semaphore_signal(barrier, inc=1, device_id=other, device_id_type=MESH)

    pairs = ((edge_hbm, edge), (proj_left_hbm, proj_left), (proj_right_hbm, proj_right))

    def load(k, i):
        part = pl.ds(i * GROUP, GROUP)
        return pltpu.make_async_copy(pairs[k][0].at[part], pairs[k][1].at[part], load_sem.at[k, i])

    lists = [
        pltpu.make_async_copy(source, target, list_sem.at[k])
        for k, (source, target) in enumerate(((order_hbm, order), (size_hbm, sizes), (sector_hbm, sectors)))
    ]
    for copy in lists:
        copy.start()
    for copy in lists:
        copy.wait()
    for i in range(STEPS):
        load(0, i).start()
    for i in range(2):
        load(1, i).start()

    pl.semaphore_wait(barrier, len(others))
    shifts = [
        pltpu.make_async_remote_copy(
            src_ref=source, dst_ref=target, send_sem=shift_send.at[k], recv_sem=shift_recv.at[k],
            device_id=sides[k], device_id_type=MESH,
        )
        for k, (source, target) in enumerate(((left_hbm, from_left), (right_hbm, from_right)))
    ]
    for copy in shifts:
        copy.start()
    plan(owner_ref, order, sizes, sectors, dest, tile_plan)
    tile_copy = pltpu.make_async_copy(tile_plan, tile_list, tile_sem)
    tile_copy.start()
    shifts[0].wait()

    left_sum[...] = jnp.zeros_like(left_sum)
    right_sum[...] = jnp.zeros_like(right_sum)

    @pl.loop(0, STEPS)
    def _(i):
        load(0, i).wait()
        load(1, i).wait()
        load(2, i).start()

        @pl.when(i < STEPS - 2)
        def _():
            load(1, i + 2).start()

        for j in range(GROUP):
            enlarged[pl.ds(j * CHI, CHI), :] = dot(from_left[...], edge[i * GROUP + j]).astype(BF16)
        chunk = proj_left[pl.ds(i * GROUP, GROUP)].reshape(GROUP * CHI, CHI)
        left_sum[...] += dot_tn(chunk, enlarged[...])
        for j in range(GROUP):
            u = i * GROUP + j
            ordered = dot(sort_matrix(dest[pl.ds(u, 1), :]), enlarged[pl.ds(j * CHI, CHI), :])
            sorted_rows[pl.ds(u * TILES, TILES)] = ordered.astype(BF16).reshape(TILES, TILE, CHI)

    def corner_copy(k):
        source, target = ((left_sum, left_other), (right_sum, right_other))[k]
        return pltpu.make_async_remote_copy(
            src_ref=source, dst_ref=target, send_sem=corner_send.at[k], recv_sem=corner_recv.at[k],
            device_id=partner, device_id_type=MESH,
        )

    corner_copy(0).start()
    shifts[1].wait()

    @pl.loop(0, STEPS)
    def _(i):
        load(2, i).wait()
        for j in range(GROUP):
            wide[:, pl.ds(j * CHI, CHI)] = dot(edge[i * GROUP + j], from_right[...]).astype(BF16)
        chunk = proj_right[pl.ds(i * GROUP, GROUP)].reshape(GROUP * CHI, CHI)
        right_sum[...] += dot(wide[...], chunk)

    corner_copy(1).start()
    tile_copy.wait()

    def result(k):
        source, target = ((left_sum, out_left), (right_sum, out_right), (gram_sum, out_gram))[k]
        return pltpu.make_async_copy(source, target, result_sem.at[k])

    def gather(listed, owner):
        for t in range(CAP_TILES):
            tile = jnp.minimum(jnp.maximum(tile_list[owner, t], 0), UNITS * TILES - 1)
            listed[pl.ds(t * TILE, TILE), :] = sorted_rows[tile]

    def packed_gram(listed):
        rows = listed[...]
        return pack(dot_tn(rows, rows))

    def mate_copy(i):
        return pltpu.make_async_remote_copy(
            src_ref=to_mate.at[i], dst_ref=from_mate.at[i], send_sem=mate_send.at[i], recv_sem=mate_recv.at[i],
            device_id=mate, device_id_type=MESH,
        )

    def row_copy(j):
        target = {"row": ((z + 1 + j // 2) % Z_CHIPS) * 2 + core}
        return pltpu.make_async_remote_copy(
            src_ref=to_row.at[j], dst_ref=from_row.at[j], send_sem=row_send.at[j], recv_sem=row_recv.at[j],
            device_id=target, device_id_type=MESH,
        )

    sec_copy = pltpu.make_async_remote_copy(
        src_ref=to_sec, dst_ref=from_sec, send_sem=sec_send, recv_sem=sec_recv,
        device_id=partner, device_id_type=MESH,
    )

    def owner_of(i, owner_core):
        return ((z + 1 + i // 2) % Z_CHIPS) * 4 + owner_core * 2 + (sec + 1 + i) % 2

    gather(listed_mate, owner_of(0, 1 - core))

    @pl.loop(0, 2 * Z_CHIPS)
    def _(i):
        to_mate[i] = packed_gram(listed_mate)
        gather(listed_mine, owner_of(i, core))
        mine[i] = packed_gram(listed_mine)
        gather(listed_mate, owner_of(i + 1, 1 - core))
        mate_copy(i).start()

        @pl.when(i >= 2)
        def _():
            mate_copy(i - 2).wait_recv()
            to_row[i - 2] = (mine[i - 2] + from_mate[i - 2]).astype(BF16)
            row_copy(i - 2).start()

    def column_sum(r):
        mate_copy(6 + r).wait_recv()
        total = mine[6 + r] + from_mate[6 + r]
        for k in range(Z_CHIPS - 1):
            row_copy(2 * k + r).wait_recv()
            total = total + from_row[2 * k + r].astype(F32)
        return total

    to_sec[...] = column_sum(0).astype(BF16)
    sec_copy.start()
    corner_copy(0).wait()
    left_sum[...] = normalized(left_sum[...] + left_other[...])
    result(0).start()
    corner_copy(1).wait()
    right_sum[...] = normalized(right_sum[...] + right_other[...])
    result(1).start()
    total = column_sum(1)
    sec_copy.wait_recv()
    gram_sum[...] = unpack(total + from_sec[...].astype(F32))
    result(2).start()
    for i in range(2 * Z_CHIPS):
        mate_copy(i).wait_send()
    for j in range(2 * (Z_CHIPS - 1)):
        row_copy(j).wait_send()
    sec_copy.wait_send()
    for k in range(3):
        result(k).wait()


def column(sector_owner, row_order, block_size, block_sector, corner_left, corner_right, edge, proj_left, proj_right):
    hbm = pl.BlockSpec(memory_space=pltpu.HBM)
    square = jax.ShapeDtypeStruct((CHI, CHI), F32)
    whole = pltpu.VMEM((UNITS, CHI, CHI), BF16)
    dma = pltpu.SemaphoreType.DMA
    return pl.pallas_call(
        column_kernel,
        in_specs=[pl.BlockSpec(memory_space=pltpu.SMEM)] + [hbm] * 8,
        out_specs=(hbm, hbm, hbm),
        out_shape=(square, square, square),
        scratch_shapes=[
            pltpu.VMEM((1, UNITS * CHI), jnp.int32),
            pltpu.VMEM((1, LANES), jnp.int32),
            pltpu.VMEM((1, LANES), jnp.int32),
            pltpu.VMEM((64, CHI), F32),
            pltpu.VMEM((OWNERS, CHI), jnp.int32),
            pltpu.SMEM((OWNERS, CHI), jnp.int32),
            pltpu.VMEM((CHI, CHI), BF16),
            pltpu.VMEM((CHI, CHI), BF16),
            whole, whole, whole,
            pltpu.VMEM((GROUP * CHI, CHI), BF16),
            pltpu.VMEM((CHI, GROUP * CHI), BF16),
            pltpu.VMEM((UNITS * TILES, TILE, CHI), BF16),
            pltpu.VMEM((CAP_TILES * TILE, CHI), BF16),
            pltpu.VMEM((CAP_TILES * TILE, CHI), BF16),
            pltpu.VMEM((CHI, CHI), F32), pltpu.VMEM((CHI, CHI), F32),
            pltpu.VMEM((CHI, CHI), F32), pltpu.VMEM((CHI, CHI), F32),
            pltpu.VMEM((CHI, CHI), F32),
            pltpu.VMEM((8, PACKED, HALF), F32),
            pltpu.VMEM((8, PACKED, HALF), F32),
            pltpu.VMEM((8, PACKED, HALF), F32),
            pltpu.VMEM((6, PACKED, HALF), BF16),
            pltpu.VMEM((6, PACKED, HALF), BF16),
            pltpu.VMEM((PACKED, HALF), BF16),
            pltpu.VMEM((PACKED, HALF), BF16),
            dma((3,)), dma, dma((2,)), dma((2,)),
            dma((3, STEPS)), dma((2,)), dma((2,)), dma((8,)), dma((8,)), dma((6,)), dma((6,)), dma, dma, dma((3,)),
        ],
        cost_estimate=pl.CostEstimate(flops=9 * 2 * 12800 * 65536, bytes_accessed=24 << 20, transcendentals=0),
        compiler_params=pltpu.CompilerParams(
            collective_id=0, has_side_effects=True, vmem_limit_bytes=58 * 1024 * 1024
        ),
    )(sector_owner, row_order, block_size, block_sector, corner_left, corner_right, edge, proj_left, proj_right)


def finish_kernel(*refs):
    held, load_sem, store_sem = refs[6:]
    loads = [pltpu.make_async_copy(refs[k], held.at[k], load_sem.at[k]) for k in range(3)]
    stores = [pltpu.make_async_copy(held.at[k], refs[3 + k], store_sem.at[k]) for k in range(3)]
    for copy in loads:
        copy.start()
    for k in range(3):
        loads[k].wait()
        stores[k].start()
    for copy in stores:
        copy.wait()


def finish(*results):
    hbm = pl.BlockSpec(memory_space=pltpu.HBM)
    square = jax.ShapeDtypeStruct((CHI, CHI), F32)
    return pl.pallas_call(
        finish_kernel,
        in_specs=[hbm] * 3,
        out_specs=(hbm,) * 3,
        out_shape=(square,) * 3,
        scratch_shapes=[
            pltpu.VMEM((3, CHI, CHI), F32), pltpu.SemaphoreType.DMA((3,)), pltpu.SemaphoreType.DMA((3,)),
        ],
        compiler_params=pltpu.CompilerParams(vmem_limit_bytes=60 * 1024 * 1024),
    )(*results)


def body(
    corner_left, corner_right, edge_top, proj_left, proj_right, row_order, block_size, block_sector, sector_owner,
):
    sums = column(
        sector_owner,
        row_order.reshape(1, UNITS * CHI),
        block_size.reshape(1, LANES),
        block_sector.reshape(1, LANES),
        corner_left[0, 0],
        corner_right[0, 0],
        jnp.transpose(edge_top[0, 0], (1, 0, 2)),
        jnp.transpose(proj_left[0, 0], (1, 0, 2)),
        proj_right[0, 0],
    )
    return tuple(out[None, None] for out in finish(*sums))


def solution(mesh):
    in_specs = (
        P("col", "row", None, None),
        P("col", "row", None, None),
        P("col", "row", None, "sec", None),
        P("col", "row", None, "sec", None),
        P("col", "row", "sec", None, None),
        P("col", "row", "sec", None),
        P("col", "row", "sec", None),
        P("col", "row", "sec", None, None),
        P(),
    )
    out_specs = (
        P("col", "row", None, None),
        P("col", "row", None, None),
        P("col", ("row", "sec"), None, None),
    )
    return jax.shard_map(body, mesh=mesh, in_specs=in_specs, out_specs=out_specs, check_vma=False)
```

```python
import functools

import jax
import jax.numpy as jnp
from jax import lax
from jax.experimental import pallas as pl
from jax.experimental.pallas import tpu as pltpu
from jax.sharding import PartitionSpec as P

CHI = 256
UNITS = 50
OWNERS = 16
LANES = 128
TILE = 16
TILES = 32
CAP_TILES = 144
EMPTY = TILES - 1
GROUP = 10
STEPS = UNITS // GROUP
HALF = 128
PACKED = 2 * HALF + TILE
Z_CHIPS = 4
EPSILON = 1e-06
MESH = pl.DeviceIdType.MESH

F32 = jnp.float32
BF16 = jnp.bfloat16


def dot(x, y):
    return lax.dot_general(x, y, (((1,), (0,)), ((), ())), preferred_element_type=F32)


def dot_nt(x, y):
    return lax.dot_general(x, y, (((1,), (1,)), ((), ())), preferred_element_type=F32)


def dot_tn(x, y):
    return lax.dot_general(x, y, (((0,), (0,)), ((), ())), preferred_element_type=F32)


def iota(shape, axis):
    return lax.broadcasted_iota(jnp.int32, shape, axis)


def ones_where(mask):
    return jnp.where(mask, 1.0, 0.0).astype(BF16)


def find_owners(owner_ref, order_ref, size_ref, sector_ref):
    sector = sector_ref[...]
    named = jnp.zeros((1, LANES), F32)
    for s in range(OWNERS):
        named = jnp.where(sector == s, (owner_ref[s] + 1).astype(F32), named)
    up = iota((LANES, LANES), 0)
    across = iota((LANES, LANES), 1)
    steps = ones_where(up == across) - ones_where(up + 1 == across)
    sizes = jnp.broadcast_to(size_ref[...].astype(F32), (TILE, LANES)).astype(BF16)
    starts = dot(sizes, ones_where(up < across))[0:1]
    delta = dot(jnp.broadcast_to(named, (TILE, LANES)).astype(BF16), steps)[0:1]
    start_hi = jnp.floor((starts + 0.5) * (1.0 / LANES))
    start_lo = starts - LANES * start_hi
    place_hi = iota((112, LANES), 0).astype(F32)
    impulses = dot_nt(
        jnp.where(place_hi == start_hi, delta, 0.0).astype(BF16),
        ones_where(up.astype(F32) == start_lo),
    ).astype(BF16)
    inside = dot(impulses, ones_where(up <= across))
    totals = jnp.broadcast_to(inside[:, LANES - 1:LANES], (112, LANES)).astype(BF16)
    listed = inside + dot(ones_where(iota((112, 112), 1) < iota((112, 112), 0)), totals)
    rows = (iota((LANES // TILE, TILE, LANES), 0) * TILE + iota((LANES // TILE, TILE, LANES), 1)).astype(F32).astype(BF16)
    one, zero = jnp.ones((), BF16), jnp.zeros((), BF16)
    halves = jnp.zeros((LANES, LANES), F32)
    for first in range(0, 100, 20):
        left, right = [], []
        for h in range(first, first + 20):
            order = order_ref[:, h * LANES:(h + 1) * LANES].astype(F32)
            pair = jnp.floor((order + 0.5) * (0.5 / UNITS))
            unit = order - 2 * UNITS * pair
            unit = jnp.where(unit >= UNITS, unit + (64 - UNITS), unit)
            pair, unit, name = (
                jnp.broadcast_to(x, (TILE, LANES)).astype(BF16)[None] for x in (pair, unit, listed[h:h + 1])
            )
            left.append(jnp.where(rows == unit, name, zero).reshape(LANES, LANES))
            right.append(jnp.where(rows == pair, one, zero).reshape(LANES, LANES))
        halves = halves + dot_nt(jnp.concatenate(left, axis=1), jnp.concatenate(right, axis=1))
    halves = halves.astype(BF16)
    up, across = iota((CHI, CHI), 0), iota((CHI, CHI), 1)
    weave = ones_where(across == jnp.where(up < LANES, 2 * up, 2 * (up - LANES) + 1))
    return dot(jnp.concatenate([halves[:64], halves[64:]], axis=1), weave)


def plan(owner_ref, order_ref, size_ref, sector_ref, dest_ref, tile_ref):
    owned = find_owners(owner_ref, order_ref, size_ref, sector_ref)
    hits = [owned == float(o + 1) for o in range(OWNERS)]
    onehot = [ones_where(hit) for hit in hits]
    ranks = dot(jnp.concatenate(onehot, axis=0), ones_where(iota((CHI, CHI), 0) <= iota((CHI, CHI), 1)))
    offset = jnp.zeros((64, 1), F32)
    dest = jnp.full((64, CHI), -1.0, F32)
    lane = iota((64, LANES), 1)
    tile_counts = jnp.zeros((64, LANES), F32)
    tile_offsets = jnp.zeros((64, LANES), F32)
    for o in range(OWNERS):
        rank = ranks[o * 64:(o + 1) * 64]
        tiles = jnp.floor((rank[:, CHI - 1:CHI] + (TILE - 1)) * (1.0 / TILE))
        dest = jnp.where(hits[o], (TILE * offset - 1.0) + rank, dest)
        tile_counts = jnp.where(lane == o, tiles, tile_counts)
        tile_offsets = jnp.where(lane == o, offset, tile_offsets)
        offset = offset + tiles
    dest_ref[...] = dest
    eye = ones_where(iota((OWNERS, LANES), 0) == iota((OWNERS, LANES), 1))
    counts = dot_nt(eye, tile_counts.astype(BF16))
    offsets = dot_nt(eye, tile_offsets.astype(BF16))
    sofar = dot(counts.astype(BF16), ones_where(iota((64, 64), 0) < iota((64, 64), 1)))
    chunk = iota((OWNERS, 64), 1)
    base = offsets - sofar + (chunk * TILES).astype(F32)
    previous = jnp.where(chunk == 0, 0.0, pltpu.roll(base, 1, 1))
    jump = base - previous
    place = iota((OWNERS, CHI), 1).astype(F32)
    tile = place
    for u in range(UNITS):
        tile = tile + jnp.where(place >= sofar[:, u:u + 1], jump[:, u:u + 1], 0.0)
    used = sofar[:, UNITS - 1:UNITS] + counts[:, UNITS - 1:UNITS]
    tile_ref[...] = jnp.where(place < used, tile, float(EMPTY)).astype(jnp.int32)


def sort_matrix(place):
    place = jnp.broadcast_to(place, (TILE, CHI))
    low = jnp.where(place < CHI, place, -1.0).astype(BF16)
    high = jnp.where(place >= CHI, place - CHI, -1.0).astype(BF16)
    rows = iota((CHI // TILE, TILE, CHI), 0) * TILE + iota((CHI // TILE, TILE, CHI), 1)
    rows = rows.astype(F32).astype(BF16)
    one, zero = jnp.ones((), BF16), jnp.zeros((), BF16)
    return jnp.concatenate(
        [jnp.where(rows == part[None], one, zero).reshape(CHI, CHI) for part in (low, high)], axis=0
    )


def pack(gram):
    upper, corner, lower = gram[:HALF, :HALF], gram[:HALF, HALF:], gram[HALF:, HALF:]
    row, col = iota((HALF, HALF), 0), iota((HALF, HALF), 1)
    diagonal = jnp.sum(jnp.where(row == col, lower, 0.0), axis=0, keepdims=True)
    return jnp.concatenate(
        [jnp.where(row <= col, upper, lower), corner, jnp.broadcast_to(diagonal, (TILE, HALF))], axis=0
    )


def unpack(packed):
    square, corner, diagonal = packed[:HALF], packed[HALF:CHI], packed[CHI:CHI + 1]
    row, col = iota((HALF, HALF), 0), iota((HALF, HALF), 1)
    turned = square.T
    upper = jnp.where(row <= col, square, turned)
    lower = jnp.where(row == col, diagonal, jnp.where(row > col, square, turned))
    return jnp.concatenate(
        [jnp.concatenate([upper, corner], axis=1), jnp.concatenate([corner.T, lower], axis=1)], axis=0
    )


def normalized(total):
    mean = jnp.sum(total * total, keepdims=True) * (1.0 / (CHI * CHI))
    return total * lax.rsqrt(mean + EPSILON)


def column_kernel(
    owner_ref, order_hbm, size_hbm, sector_hbm, left_hbm, right_hbm, edge_hbm, proj_left_hbm, proj_right_hbm,
    out_left, out_right, out_gram,
    order, sizes, sectors, dest, tile_plan, tile_list, from_left, from_right,
    edge, proj_left, proj_right, enlarged, wide, sorted_rows, listed_mate, listed_mine,
    left_sum, right_sum, left_other, right_other,
    gram_sum, mine, to_mate, from_mate, to_row, from_row,
    list_sem, tile_sem, shift_send, shift_recv, load_sem, corner_send, corner_recv, mate_send, mate_recv, row_send, row_recv, result_sem,
):
    col, row, sec = lax.axis_index("col"), lax.axis_index("row"), lax.axis_index("sec")
    z, core = row // 2, row % 2
    mate = {"row": z * 2 + (1 - core)}
    partner = {"sec": 1 - sec}
    ahead = [
        {"row": ((z + dz) % Z_CHIPS) * 2 + core, "sec": side} for dz in range(1, Z_CHIPS) for side in (sec, 1 - sec)
    ]

    sides = [{"col": (col + 1) % 8}, {"col": (col + 7) % 8}]
    others = [mate, partner] + ahead + sides

    barrier = pltpu.get_barrier_semaphore()
    for other in others:
        pl.semaphore_signal(barrier, inc=1, device_id=other, device_id_type=MESH)

    pairs = ((edge_hbm, edge), (proj_left_hbm, proj_left), (proj_right_hbm, proj_right))

    def load(k, i):
        part = pl.ds(i * GROUP, GROUP)
        return pltpu.make_async_copy(pairs[k][0].at[part], pairs[k][1].at[part], load_sem.at[k, i])

    lists = [
        pltpu.make_async_copy(source, target, list_sem.at[k])
        for k, (source, target) in enumerate(((order_hbm, order), (size_hbm, sizes), (sector_hbm, sectors)))
    ]
    for copy in lists:
        copy.start()
    shifts = [
        pltpu.make_async_remote_copy(
            src_ref=source, dst_ref=target, send_sem=shift_send.at[k], recv_sem=shift_recv.at[k],
            device_id=sides[k], device_id_type=MESH,
        )
        for k, (source, target) in enumerate(((left_hbm, from_left), (right_hbm, from_right)))
    ]
    pl.semaphore_wait(barrier, len(others))
    shifts[0].start()
    for copy in lists:
        copy.wait()
    for i in range(STEPS):
        load(0, i).start()
        if i < 2:
            load(1, i).start()

    plan(owner_ref, order, sizes, sectors, dest, tile_plan)
    shifts[1].start()
    tile_copy = pltpu.make_async_copy(tile_plan, tile_list, tile_sem)
    tile_copy.start()
    left_sum[...] = jnp.zeros_like(left_sum)
    right_sum[...] = jnp.zeros_like(right_sum)
    def corner_copy(k):
        source, target = ((left_sum, left_other), (right_sum, right_other))[k]
        return pltpu.make_async_remote_copy(
            src_ref=source, dst_ref=target, send_sem=corner_send.at[k], recv_sem=corner_recv.at[k],
            device_id=partner, device_id_type=MESH,
        )

    shifts[0].wait()

    @pl.loop(0, STEPS)
    def _(i):
        load(0, i).wait()
        load(1, i).wait()
        load(2, i).start()

        @pl.when(i < STEPS - 2)
        def _():
            load(1, i + 2).start()

        part = pl.ds(i * GROUP, GROUP)
        for j in range(GROUP):
            enlarged[i * GROUP + j] = dot(from_left[...], edge[i * GROUP + j]).astype(BF16)
        left_sum[...] += dot_tn(proj_left[part].reshape(GROUP * CHI, CHI), enlarged[part].reshape(GROUP * CHI, CHI))
        for j in range(GROUP):
            u = i * GROUP + j
            ordered = dot(sort_matrix(dest[pl.ds(u, 1), :]), enlarged[u])
            sorted_rows[pl.ds(u * TILES, TILES)] = ordered.astype(BF16).reshape(TILES, TILE, CHI)

    corner_copy(0).start()
    def result(k):
        source, target = ((left_sum, out_left), (right_sum, out_right), (gram_sum, out_gram))[k]
        return pltpu.make_async_copy(source, target, result_sem.at[k])

    def gather(listed, owner):
        for t in range(CAP_TILES):
            tile = jnp.minimum(jnp.maximum(tile_list[owner, t], 0), UNITS * TILES - 1)
            listed[pl.ds(t * TILE, TILE), :] = sorted_rows[tile]

    def packed_gram(listed):
        rows = listed[...]
        return pack(dot_tn(rows, rows))

    def mate_copy(i):
        return pltpu.make_async_remote_copy(
            src_ref=to_mate.at[i], dst_ref=from_mate.at[i], send_sem=mate_send.at[i], recv_sem=mate_recv.at[i],
            device_id=mate, device_id_type=MESH,
        )

    def row_copy(j):
        target = {"row": ((z + 1 + j) % Z_CHIPS) * 2 + core, "sec": (sec + 1 + j // Z_CHIPS) % 2}
        return pltpu.make_async_remote_copy(
            src_ref=to_row.at[j], dst_ref=from_row.at[j], send_sem=row_send.at[j], recv_sem=row_recv.at[j],
            device_id=target, device_id_type=MESH,
        )

    def owner_of(i, owner_core):
        return ((z + 1 + i) % Z_CHIPS) * 4 + owner_core * 2 + (sec + 1 + i // Z_CHIPS) % 2

    def forward(j):
        mate_copy(j).wait_recv()
        to_row[j] = (mine[j] + from_mate[j]).astype(BF16)
        row_copy(j).start()

    tile_copy.wait()
    gather(listed_mate, owner_of(0, 1 - core))
    to_mate[0] = packed_gram(listed_mate)
    gather(listed_mine, owner_of(1, 1 - core))
    mate_copy(0).start()
    to_mate[1] = packed_gram(listed_mine)
    gather(listed_mine, owner_of(0, core))
    gather(listed_mate, owner_of(2, 1 - core))
    mate_copy(1).start()

    def gram_step(i):
        mine[i] = packed_gram(listed_mine)
        gather(listed_mine, owner_of(i + 1, core))
        to_mate[i + 2] = packed_gram(listed_mate)
        gather(listed_mate, owner_of(i + 3, 1 - core))
        mate_copy(i + 2).start()
        forward(i)

    pl.loop(0, 2)(gram_step)
    shifts[1].wait()

    @pl.loop(0, STEPS)
    def _(i):
        load(2, i).wait()
        for j in range(GROUP):
            wide[:, pl.ds(j * CHI, CHI)] = dot(edge[i * GROUP + j], from_right[...]).astype(BF16)
        right_sum[...] += dot(wide[...], proj_right[pl.ds(i * GROUP, GROUP)].reshape(GROUP * CHI, CHI))

    corner_copy(1).start()
    pl.loop(2, 6)(gram_step)
    mine[6] = packed_gram(listed_mine)
    gather(listed_mate, owner_of(7, core))
    forward(6)
    mine[7] = packed_gram(listed_mate)
    corner_copy(1).wait()
    right_sum[...] = normalized(right_sum[...] + right_other[...])
    result(1).start()
    mate_copy(7).wait_recv()
    total = mine[7] + from_mate[7]
    corner_copy(0).wait()
    left_sum[...] = normalized(left_sum[...] + left_other[...])
    result(0).start()
    for j in range(7):
        row_copy(j).wait_recv()
        total = total + from_row[j].astype(F32)
    gram_sum[...] = unpack(total)
    result(2).start()
    for i in range(2 * Z_CHIPS):
        mate_copy(i).wait_send()
    for j in range(7):
        row_copy(j).wait_send()
    for k in range(3):
        result(k).wait()


def column(sector_owner, row_order, block_size, block_sector, corner_left, corner_right, edge, proj_left, proj_right):
    hbm = pl.BlockSpec(memory_space=pltpu.HBM)
    square = jax.ShapeDtypeStruct((CHI, CHI), F32)
    whole = pltpu.VMEM((UNITS, CHI, CHI), BF16)
    dma = pltpu.SemaphoreType.DMA
    return pl.pallas_call(
        column_kernel,
        in_specs=[pl.BlockSpec(memory_space=pltpu.SMEM)] + [hbm] * 8,
        out_specs=(hbm, hbm, hbm),
        out_shape=(square, square, square),
        scratch_shapes=[
            pltpu.VMEM((1, UNITS * CHI), jnp.int32),
            pltpu.VMEM((1, LANES), jnp.int32),
            pltpu.VMEM((1, LANES), jnp.int32),
            pltpu.VMEM((64, CHI), F32),
            pltpu.VMEM((OWNERS, CHI), jnp.int32),
            pltpu.SMEM((OWNERS, CHI), jnp.int32),
            pltpu.VMEM((CHI, CHI), BF16),
            pltpu.VMEM((CHI, CHI), BF16),
            whole, whole, whole, whole,
            pltpu.VMEM((CHI, GROUP * CHI), BF16),
            pltpu.VMEM((UNITS * TILES, TILE, CHI), BF16),
            pltpu.VMEM((CAP_TILES * TILE, CHI), BF16),
            pltpu.VMEM((CAP_TILES * TILE, CHI), BF16),
            pltpu.VMEM((CHI, CHI), F32), pltpu.VMEM((CHI, CHI), F32),
            pltpu.VMEM((CHI, CHI), F32), pltpu.VMEM((CHI, CHI), F32),
            pltpu.VMEM((CHI, CHI), F32),
            pltpu.VMEM((8, PACKED, HALF), F32),
            pltpu.VMEM((8, PACKED, HALF), F32),
            pltpu.VMEM((8, PACKED, HALF), F32),
            pltpu.VMEM((7, PACKED, HALF), BF16),
            pltpu.VMEM((7, PACKED, HALF), BF16),
            dma((3,)), dma, dma((2,)), dma((2,)),
            dma((3, STEPS)), dma((2,)), dma((2,)), dma((8,)), dma((8,)), dma((7,)), dma((7,)), dma((3,)),
        ],
        cost_estimate=pl.CostEstimate(flops=9 * 2 * 12800 * 65536, bytes_accessed=24 << 20, transcendentals=0),
        compiler_params=pltpu.CompilerParams(
            collective_id=0, has_side_effects=True, vmem_limit_bytes=58 * 1024 * 1024
        ),
    )(sector_owner, row_order, block_size, block_sector, corner_left, corner_right, edge, proj_left, proj_right)


def finish_kernel(*refs):
    held, load_sem, store_sem = refs[6:]
    loads = [pltpu.make_async_copy(refs[k], held.at[k], load_sem.at[k]) for k in range(3)]
    stores = [pltpu.make_async_copy(held.at[k], refs[3 + k], store_sem.at[k]) for k in range(3)]
    for copy in loads:
        copy.start()
    for k in range(3):
        loads[k].wait()
        stores[k].start()
    for copy in stores:
        copy.wait()


def finish(*results):
    hbm = pl.BlockSpec(memory_space=pltpu.HBM)
    square = jax.ShapeDtypeStruct((CHI, CHI), F32)
    return pl.pallas_call(
        finish_kernel,
        in_specs=[hbm] * 3,
        out_specs=(hbm,) * 3,
        out_shape=(square,) * 3,
        scratch_shapes=[
            pltpu.VMEM((3, CHI, CHI), F32), pltpu.SemaphoreType.DMA((3,)), pltpu.SemaphoreType.DMA((3,)),
        ],
        compiler_params=pltpu.CompilerParams(vmem_limit_bytes=60 * 1024 * 1024),
    )(*results)


def body(
    corner_left, corner_right, edge_top, proj_left, proj_right, row_order, block_size, block_sector, sector_owner,
):
    sums = column(
        sector_owner,
        row_order.reshape(1, UNITS * CHI),
        block_size.reshape(1, LANES),
        block_sector.reshape(1, LANES),
        corner_left[0, 0],
        corner_right[0, 0],
        jnp.transpose(edge_top[0, 0], (1, 0, 2)),
        jnp.transpose(proj_left[0, 0], (1, 0, 2)),
        proj_right[0, 0],
    )
    return tuple(out[None, None] for out in finish(*sums))


def solution(mesh):
    in_specs = (
        P("col", "row", None, None),
        P("col", "row", None, None),
        P("col", "row", None, "sec", None),
        P("col", "row", None, "sec", None),
        P("col", "row", "sec", None, None),
        P("col", "row", "sec", None),
        P("col", "row", "sec", None),
        P("col", "row", "sec", None, None),
        P(),
    )
    out_specs = (
        P("col", "row", None, None),
        P("col", "row", None, None),
        P("col", ("row", "sec"), None, None),
    )
    return jax.shard_map(body, mesh=mesh, in_specs=in_specs, out_specs=out_specs, check_vma=False)
```

```python
import functools

import jax
import jax.numpy as jnp
from jax import lax
from jax.experimental import pallas as pl
from jax.experimental.pallas import tpu as pltpu
from jax.sharding import PartitionSpec as P

CHI = 256
UNITS = 50
OWNERS = 16
LANES = 128
TILE = 16
TILES = 32
CAP_TILES = 144
HELD = 2048
EMPTY = TILES - 1
GROUP = 10
STEPS = UNITS // GROUP
HALF = 128
PACKED = 2 * HALF + TILE
Z_CHIPS = 4
EPSILON = 1e-06
MESH = pl.DeviceIdType.MESH

F32 = jnp.float32
BF16 = jnp.bfloat16


def dot(x, y):
    return lax.dot_general(x, y, (((1,), (0,)), ((), ())), preferred_element_type=F32)


def dot_nt(x, y):
    return lax.dot_general(x, y, (((1,), (1,)), ((), ())), preferred_element_type=F32)


def dot_tn(x, y):
    return lax.dot_general(x, y, (((0,), (0,)), ((), ())), preferred_element_type=F32)


def iota(shape, axis):
    return lax.broadcasted_iota(jnp.int32, shape, axis)


def ones_where(mask):
    return jnp.where(mask, 1.0, 0.0).astype(BF16)


def find_owners(owner_ref, order_ref, size_ref, sector_ref):
    sector = sector_ref[...]
    named = jnp.zeros((1, LANES), F32)
    for s in range(OWNERS):
        named = jnp.where(sector == s, (owner_ref[s] + 1).astype(F32), named)
    up = iota((LANES, LANES), 0)
    across = iota((LANES, LANES), 1)
    steps = ones_where(up == across) - ones_where(up + 1 == across)
    sizes = jnp.broadcast_to(size_ref[...].astype(F32), (TILE, LANES)).astype(BF16)
    starts = dot(sizes, ones_where(up < across))[0:1]
    delta = dot(jnp.broadcast_to(named, (TILE, LANES)).astype(BF16), steps)[0:1]
    start_hi = jnp.floor((starts + 0.5) * (1.0 / LANES))
    start_lo = starts - LANES * start_hi
    place_hi = iota((112, LANES), 0).astype(F32)
    impulses = dot_nt(
        jnp.where(place_hi == start_hi, delta, 0.0).astype(BF16),
        ones_where(up.astype(F32) == start_lo),
    ).astype(BF16)
    inside = dot(impulses, ones_where(up <= across))
    totals = jnp.broadcast_to(inside[:, LANES - 1:LANES], (112, LANES)).astype(BF16)
    listed = inside + dot(ones_where(iota((112, 112), 1) < iota((112, 112), 0)), totals)
    rows = (iota((LANES // TILE, TILE, LANES), 0) * TILE + iota((LANES // TILE, TILE, LANES), 1)).astype(F32).astype(BF16)
    one, zero = jnp.ones((), BF16), jnp.zeros((), BF16)
    halves = jnp.zeros((LANES, LANES), F32)
    for first in range(0, 100, 20):
        left, right = [], []
        for h in range(first, first + 20):
            order = order_ref[:, h * LANES:(h + 1) * LANES].astype(F32)
            pair = jnp.floor((order + 0.5) * (0.5 / UNITS))
            unit = order - 2 * UNITS * pair
            unit = jnp.where(unit >= UNITS, unit + (64 - UNITS), unit)
            pair, unit, name = (
                jnp.broadcast_to(x, (TILE, LANES)).astype(BF16)[None] for x in (pair, unit, listed[h:h + 1])
            )
            left.append(jnp.where(rows == unit, name, zero).reshape(LANES, LANES))
            right.append(jnp.where(rows == pair, one, zero).reshape(LANES, LANES))
        halves = halves + dot_nt(jnp.concatenate(left, axis=1), jnp.concatenate(right, axis=1))
    halves = halves.astype(BF16)
    up, across = iota((CHI, CHI), 0), iota((CHI, CHI), 1)
    weave = ones_where(across == jnp.where(up < LANES, 2 * up, 2 * (up - LANES) + 1))
    return dot(jnp.concatenate([halves[:64], halves[64:]], axis=1), weave)


def plan(owner_ref, order_ref, size_ref, sector_ref, dest_ref, tile_ref):
    owned = find_owners(owner_ref, order_ref, size_ref, sector_ref)
    hits = [owned == float(o + 1) for o in range(OWNERS)]
    onehot = [ones_where(hit) for hit in hits]
    ranks = dot(jnp.concatenate(onehot, axis=0), ones_where(iota((CHI, CHI), 0) <= iota((CHI, CHI), 1)))
    offset = jnp.zeros((64, 1), F32)
    dest = jnp.full((64, CHI), -1.0, F32)
    lane = iota((64, LANES), 1)
    tile_counts = jnp.zeros((64, LANES), F32)
    tile_offsets = jnp.zeros((64, LANES), F32)
    for o in range(OWNERS):
        rank = ranks[o * 64:(o + 1) * 64]
        tiles = jnp.floor((rank[:, CHI - 1:CHI] + (TILE - 1)) * (1.0 / TILE))
        dest = jnp.where(hits[o], (TILE * offset - 1.0) + rank, dest)
        tile_counts = jnp.where(lane == o, tiles, tile_counts)
        tile_offsets = jnp.where(lane == o, offset, tile_offsets)
        offset = offset + tiles
    dest_ref[...] = dest
    eye = ones_where(iota((OWNERS, LANES), 0) == iota((OWNERS, LANES), 1))
    counts = dot_nt(eye, tile_counts.astype(BF16))
    offsets = dot_nt(eye, tile_offsets.astype(BF16))
    sofar = dot(counts.astype(BF16), ones_where(iota((64, 64), 0) < iota((64, 64), 1)))
    chunk = iota((OWNERS, 64), 1)
    base = offsets - sofar + (chunk * TILES).astype(F32)
    previous = jnp.where(chunk == 0, 0.0, pltpu.roll(base, 1, 1))
    jump = base - previous
    place = iota((OWNERS, CHI), 1).astype(F32)
    tile = place
    for u in range(UNITS):
        tile = tile + jnp.where(place >= sofar[:, u:u + 1], jump[:, u:u + 1], 0.0)
    used = sofar[:, UNITS - 1:UNITS] + counts[:, UNITS - 1:UNITS]
    tile_ref[...] = jnp.where(place < used, tile, float(EMPTY)).astype(jnp.int32)


def sort_matrix(place):
    place = jnp.broadcast_to(place, (TILE, CHI))
    low = jnp.where(place < CHI, place, -1.0).astype(BF16)
    high = jnp.where(place >= CHI, place - CHI, -1.0).astype(BF16)
    rows = iota((CHI // TILE, TILE, CHI), 0) * TILE + iota((CHI // TILE, TILE, CHI), 1)
    rows = rows.astype(F32).astype(BF16)
    one, zero = jnp.ones((), BF16), jnp.zeros((), BF16)
    return jnp.concatenate(
        [jnp.where(rows == part[None], one, zero).reshape(CHI, CHI) for part in (low, high)], axis=0
    )


def pack(gram):
    upper, corner, lower = gram[:HALF, :HALF], gram[:HALF, HALF:], gram[HALF:, HALF:]
    row, col = iota((HALF, HALF), 0), iota((HALF, HALF), 1)
    diagonal = jnp.sum(jnp.where(row == col, lower, 0.0), axis=0, keepdims=True)
    return jnp.concatenate(
        [jnp.where(row <= col, upper, lower), corner, jnp.broadcast_to(diagonal, (TILE, HALF))], axis=0
    )


def unpack(packed):
    square, corner, diagonal = packed[:HALF], packed[HALF:CHI], packed[CHI:CHI + 1]
    row, col = iota((HALF, HALF), 0), iota((HALF, HALF), 1)
    turned = square.T
    upper = jnp.where(row <= col, square, turned)
    lower = jnp.where(row == col, diagonal, jnp.where(row > col, square, turned))
    return jnp.concatenate(
        [jnp.concatenate([upper, corner], axis=1), jnp.concatenate([corner.T, lower], axis=1)], axis=0
    )


def normalized(total):
    mean = jnp.sum(total * total, keepdims=True) * (1.0 / (CHI * CHI))
    return total * lax.rsqrt(mean + EPSILON)


def column_kernel(
    owner_ref, order_hbm, size_hbm, sector_hbm, left_hbm, right_hbm, edge_hbm, proj_left_hbm, proj_right_hbm,
    out_left, out_right, out_gram,
    order, sizes, sectors, dest, tile_plan, tile_list, from_left, from_right,
    edge, proj_left, proj_right, enlarged, wide, sorted_rows, listed_mate, listed_mine,
    left_sum, right_sum, left_other, right_other,
    gram_sum, mine, to_mate, from_mate, to_row, from_row,
    list_sem, tile_sem, shift_send, shift_recv, load_sem, corner_send, corner_recv, mate_send, mate_recv, row_send, row_recv, result_sem,
):
    col, row, sec = lax.axis_index("col"), lax.axis_index("row"), lax.axis_index("sec")
    z, core = row // 2, row % 2
    mate = {"row": z * 2 + (1 - core)}
    partner = {"sec": 1 - sec}
    ahead = [
        {"row": ((z + dz) % Z_CHIPS) * 2 + core, "sec": side} for dz in range(1, Z_CHIPS) for side in (sec, 1 - sec)
    ]

    sides = [{"col": (col + 1) % 8}, {"col": (col + 7) % 8}]
    others = sides + [mate, partner] + ahead

    barrier = pltpu.get_barrier_semaphore()
    for other in others:
        pl.semaphore_signal(barrier, inc=1, device_id=other, device_id_type=MESH)

    pairs = ((edge_hbm, edge), (proj_left_hbm, proj_left), (proj_right_hbm, proj_right))

    def load(k, i):
        part = pl.ds(i * GROUP, GROUP)
        return pltpu.make_async_copy(pairs[k][0].at[part], pairs[k][1].at[part], load_sem.at[k, i])

    lists = [
        pltpu.make_async_copy(source, target, list_sem.at[k])
        for k, (source, target) in enumerate(((order_hbm, order), (size_hbm, sizes), (sector_hbm, sectors)))
    ]
    for copy in lists:
        copy.start()
    shifts = [
        pltpu.make_async_remote_copy(
            src_ref=source, dst_ref=target, send_sem=shift_send.at[k], recv_sem=shift_recv.at[k],
            device_id=sides[k], device_id_type=MESH,
        )
        for k, (source, target) in enumerate(((left_hbm, from_left), (right_hbm, from_right)))
    ]
    pl.semaphore_wait(barrier, len(others))
    shifts[0].start()
    for copy in lists:
        copy.wait()
    for i in range(STEPS):
        load(0, i).start()
        if i < 2:
            load(1, i).start()

    plan(owner_ref, order, sizes, sectors, dest, tile_plan)
    shifts[1].start()
    tile_copy = pltpu.make_async_copy(tile_plan, tile_list, tile_sem)
    tile_copy.start()
    left_sum[...] = jnp.zeros_like(left_sum)
    right_sum[...] = jnp.zeros_like(right_sum)
    def corner_copy(k):
        source, target = ((left_sum, left_other), (right_sum, right_other))[k]
        return pltpu.make_async_remote_copy(
            src_ref=source, dst_ref=target, send_sem=corner_send.at[k], recv_sem=corner_recv.at[k],
            device_id=partner, device_id_type=MESH,
        )

    shifts[0].wait()

    @pl.loop(0, STEPS)
    def _(i):
        load(0, i).wait()
        load(1, i).wait()
        load(2, i).start()

        @pl.when(i < STEPS - 2)
        def _():
            load(1, i + 2).start()

        part = pl.ds(i * GROUP, GROUP)
        for j in range(GROUP):
            enlarged[i * GROUP + j] = dot(from_left[...], edge[i * GROUP + j]).astype(BF16)
        left_sum[...] += dot_tn(proj_left[part].reshape(GROUP * CHI, CHI), enlarged[part].reshape(GROUP * CHI, CHI))
        for j in range(GROUP):
            u = i * GROUP + j
            ordered = dot(sort_matrix(dest[pl.ds(u, 1), :]), enlarged[u])
            sorted_rows[pl.ds(u * TILES, TILES)] = ordered.astype(BF16).reshape(TILES, TILE, CHI)

    corner_copy(0).start()
    def result(k):
        source, target = ((left_sum, out_left), (right_sum, out_right), (gram_sum, out_gram))[k]
        return pltpu.make_async_copy(source, target, result_sem.at[k])

    def gather(listed, owner):
        for t in range(CAP_TILES):
            tile = tile_list[owner, t] & (HELD - 1)
            listed[pl.ds(t * TILE, TILE), :] = sorted_rows[tile]

    def packed_gram(listed):
        rows = listed[...]
        return pack(dot_tn(rows, rows))

    def mate_copy(i):
        return pltpu.make_async_remote_copy(
            src_ref=to_mate.at[i], dst_ref=from_mate.at[i], send_sem=mate_send.at[i], recv_sem=mate_recv.at[i],
            device_id=mate, device_id_type=MESH,
        )

    def row_copy(j):
        target = {"row": ((z + 1 + j) % Z_CHIPS) * 2 + core, "sec": (sec + 1 + j // Z_CHIPS) % 2}
        return pltpu.make_async_remote_copy(
            src_ref=to_row.at[j], dst_ref=from_row.at[j], send_sem=row_send.at[j], recv_sem=row_recv.at[j],
            device_id=target, device_id_type=MESH,
        )

    def owner_of(i, owner_core):
        return ((z + 1 + i) % Z_CHIPS) * 4 + owner_core * 2 + (sec + 1 + i // Z_CHIPS) % 2

    def forward(j):
        mate_copy(j).wait_recv()
        to_row[j] = (mine[j] + from_mate[j]).astype(BF16)
        row_copy(j).start()

    tile_copy.wait()
    gather(listed_mate, owner_of(0, 1 - core))
    to_mate[0] = packed_gram(listed_mate)
    gather(listed_mine, owner_of(1, 1 - core))
    mate_copy(0).start()
    to_mate[1] = packed_gram(listed_mine)
    gather(listed_mine, owner_of(0, core))
    gather(listed_mate, owner_of(2, 1 - core))
    mate_copy(1).start()

    def gram_step(i):
        mine[i] = packed_gram(listed_mine)
        gather(listed_mine, owner_of(i + 1, core))
        to_mate[i + 2] = packed_gram(listed_mate)
        gather(listed_mate, owner_of(i + 3, 1 - core))
        mate_copy(i + 2).start()
        forward(i)

    pl.loop(0, 4)(gram_step)
    shifts[1].wait()

    @pl.loop(0, STEPS)
    def _(i):
        load(2, i).wait()
        for j in range(GROUP):
            wide[:, pl.ds(j * CHI, CHI)] = dot(edge[i * GROUP + j], from_right[...]).astype(BF16)
        right_sum[...] += dot(wide[...], proj_right[pl.ds(i * GROUP, GROUP)].reshape(GROUP * CHI, CHI))

    corner_copy(1).start()
    pl.loop(4, 6)(gram_step)
    mine[6] = packed_gram(listed_mine)
    gather(listed_mate, owner_of(7, core))
    forward(6)
    mine[7] = packed_gram(listed_mate)
    corner_copy(1).wait()
    right_sum[...] = normalized(right_sum[...] + right_other[...])
    result(1).start()
    mate_copy(7).wait_recv()
    total = mine[7] + from_mate[7]
    corner_copy(0).wait()
    left_sum[...] = normalized(left_sum[...] + left_other[...])
    result(0).start()
    for j in range(7):
        row_copy(j).wait_recv()
        total = total + from_row[j].astype(F32)
    gram_sum[...] = unpack(total)
    result(2).start()
    for i in range(2 * Z_CHIPS):
        mate_copy(i).wait_send()
    for j in range(7):
        row_copy(j).wait_send()
    for k in range(3):
        result(k).wait()


def column(sector_owner, row_order, block_size, block_sector, corner_left, corner_right, edge, proj_left, proj_right):
    hbm = pl.BlockSpec(memory_space=pltpu.HBM)
    square = jax.ShapeDtypeStruct((CHI, CHI), F32)
    whole = pltpu.VMEM((UNITS, CHI, CHI), BF16)
    dma = pltpu.SemaphoreType.DMA
    return pl.pallas_call(
        column_kernel,
        in_specs=[pl.BlockSpec(memory_space=pltpu.SMEM)] + [hbm] * 8,
        out_specs=(hbm, hbm, hbm),
        out_shape=(square, square, square),
        scratch_shapes=[
            pltpu.VMEM((1, UNITS * CHI), jnp.int32),
            pltpu.VMEM((1, LANES), jnp.int32),
            pltpu.VMEM((1, LANES), jnp.int32),
            pltpu.VMEM((64, CHI), F32),
            pltpu.VMEM((OWNERS, CHI), jnp.int32),
            pltpu.SMEM((OWNERS, CHI), jnp.int32),
            pltpu.VMEM((CHI, CHI), BF16),
            pltpu.VMEM((CHI, CHI), BF16),
            whole, whole, whole, whole,
            pltpu.VMEM((CHI, GROUP * CHI), BF16),
            pltpu.VMEM((HELD, TILE, CHI), BF16),
            pltpu.VMEM((CAP_TILES * TILE, CHI), BF16),
            pltpu.VMEM((CAP_TILES * TILE, CHI), BF16),
            pltpu.VMEM((CHI, CHI), F32), pltpu.VMEM((CHI, CHI), F32),
            pltpu.VMEM((CHI, CHI), F32), pltpu.VMEM((CHI, CHI), F32),
            pltpu.VMEM((CHI, CHI), F32),
            pltpu.VMEM((8, PACKED, HALF), F32),
            pltpu.VMEM((8, PACKED, HALF), F32),
            pltpu.VMEM((8, PACKED, HALF), F32),
            pltpu.VMEM((7, PACKED, HALF), BF16),
            pltpu.VMEM((7, PACKED, HALF), BF16),
            dma((3,)), dma, dma((2,)), dma((2,)),
            dma((3, STEPS)), dma((2,)), dma((2,)), dma((8,)), dma((8,)), dma((7,)), dma((7,)), dma((3,)),
        ],
        cost_estimate=pl.CostEstimate(flops=9 * 2 * 12800 * 65536, bytes_accessed=24 << 20, transcendentals=0),
        compiler_params=pltpu.CompilerParams(
            collective_id=0, has_side_effects=True, vmem_limit_bytes=58 * 1024 * 1024
        ),
    )(sector_owner, row_order, block_size, block_sector, corner_left, corner_right, edge, proj_left, proj_right)


def finish_kernel(*refs):
    held, load_sem, store_sem = refs[6:]
    loads = [pltpu.make_async_copy(refs[k], held.at[k], load_sem.at[k]) for k in range(3)]
    stores = [pltpu.make_async_copy(held.at[k], refs[3 + k], store_sem.at[k]) for k in range(3)]
    for copy in loads:
        copy.start()
    for k in range(3):
        loads[k].wait()
        stores[k].start()
    for copy in stores:
        copy.wait()


def finish(*results):
    hbm = pl.BlockSpec(memory_space=pltpu.HBM)
    square = jax.ShapeDtypeStruct((CHI, CHI), F32)
    return pl.pallas_call(
        finish_kernel,
        in_specs=[hbm] * 3,
        out_specs=(hbm,) * 3,
        out_shape=(square,) * 3,
        scratch_shapes=[
            pltpu.VMEM((3, CHI, CHI), F32), pltpu.SemaphoreType.DMA((3,)), pltpu.SemaphoreType.DMA((3,)),
        ],
        compiler_params=pltpu.CompilerParams(vmem_limit_bytes=60 * 1024 * 1024),
    )(*results)


def body(
    corner_left, corner_right, edge_top, proj_left, proj_right, row_order, block_size, block_sector, sector_owner,
):
    sums = column(
        sector_owner,
        row_order.reshape(1, UNITS * CHI),
        block_size.reshape(1, LANES),
        block_sector.reshape(1, LANES),
        corner_left[0, 0],
        corner_right[0, 0],
        jnp.transpose(edge_top[0, 0], (1, 0, 2)),
        jnp.transpose(proj_left[0, 0], (1, 0, 2)),
        proj_right[0, 0],
    )
    return tuple(out[None, None] for out in finish(*sums))


def solution(mesh):
    in_specs = (
        P("col", "row", None, None),
        P("col", "row", None, None),
        P("col", "row", None, "sec", None),
        P("col", "row", None, "sec", None),
        P("col", "row", "sec", None, None),
        P("col", "row", "sec", None),
        P("col", "row", "sec", None),
        P("col", "row", "sec", None, None),
        P(),
    )
    out_specs = (
        P("col", "row", None, None),
        P("col", "row", None, None),
        P("col", ("row", "sec"), None, None),
    )
    return jax.shard_map(body, mesh=mesh, in_specs=in_specs, out_specs=out_specs, check_vma=False)
```

```python
import functools

import jax
import jax.numpy as jnp
from jax import lax
from jax.experimental import pallas as pl
from jax.experimental.pallas import tpu as pltpu
from jax.sharding import PartitionSpec as P

CHI = 256
UNITS = 50
OWNERS = 16
LANES = 128
TILE = 16
TILES = 32
CAP_TILES = 144
EMPTY = TILES - 1
GROUP = 10
STEPS = UNITS // GROUP
HALF = 128
PACKED = 2 * HALF + TILE
Z_CHIPS = 4
EPSILON = 1e-06
MESH = pl.DeviceIdType.MESH

F32 = jnp.float32
BF16 = jnp.bfloat16


def dot(x, y):
    return lax.dot_general(x, y, (((1,), (0,)), ((), ())), preferred_element_type=F32)


def dot_nt(x, y):
    return lax.dot_general(x, y, (((1,), (1,)), ((), ())), preferred_element_type=F32)


def dot_tn(x, y):
    return lax.dot_general(x, y, (((0,), (0,)), ((), ())), preferred_element_type=F32)


def iota(shape, axis):
    return lax.broadcasted_iota(jnp.int32, shape, axis)


def ones_where(mask):
    return jnp.where(mask, 1.0, 0.0).astype(BF16)


def find_owners(owner_ref, order_ref, size_ref, sector_ref):
    sector = sector_ref[...]
    named = jnp.zeros((1, LANES), F32)
    for s in range(OWNERS):
        named = jnp.where(sector == s, (owner_ref[s] + 1).astype(F32), named)
    up = iota((LANES, LANES), 0)
    across = iota((LANES, LANES), 1)
    steps = ones_where(up == across) - ones_where(up + 1 == across)
    sizes = jnp.broadcast_to(size_ref[...].astype(F32), (TILE, LANES)).astype(BF16)
    starts = dot(sizes, ones_where(up < across))[0:1]
    delta = dot(jnp.broadcast_to(named, (TILE, LANES)).astype(BF16), steps)[0:1]
    start_hi = jnp.floor((starts + 0.5) * (1.0 / LANES))
    start_lo = starts - LANES * start_hi
    place_hi = iota((112, LANES), 0).astype(F32)
    impulses = dot_nt(
        jnp.where(place_hi == start_hi, delta, 0.0).astype(BF16),
        ones_where(up.astype(F32) == start_lo),
    ).astype(BF16)
    inside = dot(impulses, ones_where(up <= across))
    totals = jnp.broadcast_to(inside[:, LANES - 1:LANES], (112, LANES)).astype(BF16)
    listed = inside + dot(ones_where(iota((112, 112), 1) < iota((112, 112), 0)), totals)
    rows = (iota((LANES // TILE, TILE, LANES), 0) * TILE + iota((LANES // TILE, TILE, LANES), 1)).astype(F32).astype(BF16)
    one, zero = jnp.ones((), BF16), jnp.zeros((), BF16)
    halves = jnp.zeros((LANES, LANES), F32)
    for first in range(0, 100, 20):
        left, right = [], []
        for h in range(first, first + 20):
            order = order_ref[:, h * LANES:(h + 1) * LANES].astype(F32)
            pair = jnp.floor((order + 0.5) * (0.5 / UNITS))
            unit = order - 2 * UNITS * pair
            unit = jnp.where(unit >= UNITS, unit + (64 - UNITS), unit)
            pair, unit, name = (
                jnp.broadcast_to(x, (TILE, LANES)).astype(BF16)[None] for x in (pair, unit, listed[h:h + 1])
            )
            left.append(jnp.where(rows == unit, name, zero).reshape(LANES, LANES))
            right.append(jnp.where(rows == pair, one, zero).reshape(LANES, LANES))
        halves = halves + dot_nt(jnp.concatenate(left, axis=1), jnp.concatenate(right, axis=1))
    halves = halves.astype(BF16)
    up, across = iota((CHI, CHI), 0), iota((CHI, CHI), 1)
    weave = ones_where(across == jnp.where(up < LANES, 2 * up, 2 * (up - LANES) + 1))
    return dot(jnp.concatenate([halves[:64], halves[64:]], axis=1), weave)


def plan(owner_ref, order_ref, size_ref, sector_ref, dest_ref, tile_ref):
    owned = find_owners(owner_ref, order_ref, size_ref, sector_ref)
    hits = [owned == float(o + 1) for o in range(OWNERS)]
    onehot = [ones_where(hit) for hit in hits]
    ranks = dot(jnp.concatenate(onehot, axis=0), ones_where(iota((CHI, CHI), 0) <= iota((CHI, CHI), 1)))
    offset = jnp.zeros((64, 1), F32)
    dest = jnp.full((64, CHI), -1.0, F32)
    lane = iota((64, LANES), 1)
    tile_counts = jnp.zeros((64, LANES), F32)
    tile_offsets = jnp.zeros((64, LANES), F32)
    for o in range(OWNERS):
        rank = ranks[o * 64:(o + 1) * 64]
        tiles = jnp.floor((rank[:, CHI - 1:CHI] + (TILE - 1)) * (1.0 / TILE))
        dest = jnp.where(hits[o], (TILE * offset - 1.0) + rank, dest)
        tile_counts = jnp.where(lane == o, tiles, tile_counts)
        tile_offsets = jnp.where(lane == o, offset, tile_offsets)
        offset = offset + tiles
    dest_ref[...] = dest
    eye = ones_where(iota((OWNERS, LANES), 0) == iota((OWNERS, LANES), 1))
    counts = dot_nt(eye, tile_counts.astype(BF16))
    offsets = dot_nt(eye, tile_offsets.astype(BF16))
    sofar = dot(counts.astype(BF16), ones_where(iota((64, 64), 0) < iota((64, 64), 1)))
    chunk = iota((OWNERS, 64), 1)
    base = offsets - sofar + (chunk * TILES).astype(F32)
    previous = jnp.where(chunk == 0, 0.0, pltpu.roll(base, 1, 1))
    jump = base - previous
    place = iota((OWNERS, CHI), 1).astype(F32)
    tile = place
    for u in range(UNITS):
        tile = tile + jnp.where(place >= sofar[:, u:u + 1], jump[:, u:u + 1], 0.0)
    used = sofar[:, UNITS - 1:UNITS] + counts[:, UNITS - 1:UNITS]
    tile_ref[...] = jnp.where(place < used, tile, float(EMPTY)).astype(jnp.int32)


def sort_matrix(place):
    place = jnp.broadcast_to(place, (TILE, CHI))
    low = jnp.where(place < CHI, place, -1.0).astype(BF16)
    high = jnp.where(place >= CHI, place - CHI, -1.0).astype(BF16)
    rows = iota((CHI // TILE, TILE, CHI), 0) * TILE + iota((CHI // TILE, TILE, CHI), 1)
    rows = rows.astype(F32).astype(BF16)
    one, zero = jnp.ones((), BF16), jnp.zeros((), BF16)
    return jnp.concatenate(
        [jnp.where(rows == part[None], one, zero).reshape(CHI, CHI) for part in (low, high)], axis=0
    )


def pack(gram):
    upper, corner, lower = gram[:HALF, :HALF], gram[:HALF, HALF:], gram[HALF:, HALF:]
    row, col = iota((HALF, HALF), 0), iota((HALF, HALF), 1)
    diagonal = jnp.sum(jnp.where(row == col, lower, 0.0), axis=0, keepdims=True)
    return jnp.concatenate(
        [jnp.where(row <= col, upper, lower), corner, jnp.broadcast_to(diagonal, (TILE, HALF))], axis=0
    )


def unpack(packed):
    square, corner, diagonal = packed[:HALF], packed[HALF:CHI], packed[CHI:CHI + 1]
    row, col = iota((HALF, HALF), 0), iota((HALF, HALF), 1)
    turned = square.T
    upper = jnp.where(row <= col, square, turned)
    lower = jnp.where(row == col, diagonal, jnp.where(row > col, square, turned))
    return jnp.concatenate(
        [jnp.concatenate([upper, corner], axis=1), jnp.concatenate([corner.T, lower], axis=1)], axis=0
    )


def normalized(total):
    mean = jnp.sum(total * total, keepdims=True) * (1.0 / (CHI * CHI))
    return total * lax.rsqrt(mean + EPSILON)


def column_kernel(
    owner_ref, order_hbm, size_hbm, sector_hbm, left_hbm, right_hbm, edge_hbm, proj_left_hbm, proj_right_hbm,
    out_left, out_right, out_gram,
    order, sizes, sectors, dest, tile_plan, tile_list, from_left, from_right,
    edge, proj_left, proj_right, enlarged, wide, sorted_rows, listed_mate, listed_mine,
    left_sum, right_sum, left_other, right_other,
    gram_sum, mine, to_mate, from_mate, to_row, from_row,
    list_sem, tile_sem, shift_send, shift_recv, load_sem, corner_send, corner_recv, mate_send, mate_recv, row_send, row_recv, result_sem,
):
    col, row, sec = lax.axis_index("col"), lax.axis_index("row"), lax.axis_index("sec")
    z, core = row // 2, row % 2
    mate = {"row": z * 2 + (1 - core)}
    partner = {"sec": 1 - sec}
    ahead = [
        {"row": ((z + dz) % Z_CHIPS) * 2 + core, "sec": side} for dz in range(1, Z_CHIPS) for side in (sec, 1 - sec)
    ]

    sides = [{"col": (col + 1) % 8}, {"col": (col + 7) % 8}]
    others = [mate, partner] + ahead + sides

    barrier = pltpu.get_barrier_semaphore()
    for other in others:
        pl.semaphore_signal(barrier, inc=1, device_id=other, device_id_type=MESH)

    pairs = ((edge_hbm, edge), (proj_left_hbm, proj_left), (proj_right_hbm, proj_right))

    def load(k, i):
        part = pl.ds(i * GROUP, GROUP)
        return pltpu.make_async_copy(pairs[k][0].at[part], pairs[k][1].at[part], load_sem.at[k, i])

    lists = [
        pltpu.make_async_copy(source, target, list_sem.at[k])
        for k, (source, target) in enumerate(((order_hbm, order), (size_hbm, sizes), (sector_hbm, sectors)))
    ]
    for copy in lists:
        copy.start()
    shifts = [
        pltpu.make_async_remote_copy(
            src_ref=source, dst_ref=target, send_sem=shift_send.at[k], recv_sem=shift_recv.at[k],
            device_id=sides[k], device_id_type=MESH,
        )
        for k, (source, target) in enumerate(((left_hbm, from_left), (right_hbm, from_right)))
    ]
    pl.semaphore_wait(barrier, len(others))
    shifts[0].start()
    for copy in lists:
        copy.wait()
    for i in range(STEPS):
        load(0, i).start()
        if i < 2:
            load(1, i).start()

    plan(owner_ref, order, sizes, sectors, dest, tile_plan)
    shifts[1].start()
    tile_copy = pltpu.make_async_copy(tile_plan, tile_list, tile_sem)
    tile_copy.start()
    left_sum[...] = jnp.zeros_like(left_sum)
    right_sum[...] = jnp.zeros_like(right_sum)
    def corner_copy(k):
        source, target = ((left_sum, left_other), (right_sum, right_other))[k]
        return pltpu.make_async_remote_copy(
            src_ref=source, dst_ref=target, send_sem=corner_send.at[k], recv_sem=corner_recv.at[k],
            device_id=partner, device_id_type=MESH,
        )

    shifts[0].wait()

    @pl.loop(0, STEPS)
    def _(i):
        load(0, i).wait()
        load(1, i).wait()
        load(2, i).start()

        @pl.when(i < STEPS - 2)
        def _():
            load(1, i + 2).start()

        part = pl.ds(i * GROUP, GROUP)
        for j in range(GROUP):
            enlarged[i * GROUP + j] = dot(from_left[...], edge[i * GROUP + j]).astype(BF16)
        left_sum[...] += dot_tn(proj_left[part].reshape(GROUP * CHI, CHI), enlarged[part].reshape(GROUP * CHI, CHI))
        for j in range(GROUP):
            u = i * GROUP + j
            ordered = dot(sort_matrix(dest[pl.ds(u, 1), :]), enlarged[u])
            sorted_rows[pl.ds(u * TILES, TILES)] = ordered.astype(BF16).reshape(TILES, TILE, CHI)

    corner_copy(0).start()
    def result(k):
        source, target = ((left_sum, out_left), (right_sum, out_right), (gram_sum, out_gram))[k]
        return pltpu.make_async_copy(source, target, result_sem.at[k])

    def gather(listed, owner):
        for t in range(CAP_TILES):
            tile = jnp.minimum(jnp.maximum(tile_list[owner, t], 0), UNITS * TILES - 1)
            listed[pl.ds(t * TILE, TILE), :] = sorted_rows[tile]

    def packed_gram(listed):
        rows = listed[...]
        return pack(dot_tn(rows, rows))

    def mate_copy(i):
        return pltpu.make_async_remote_copy(
            src_ref=to_mate.at[i], dst_ref=from_mate.at[i], send_sem=mate_send.at[i], recv_sem=mate_recv.at[i],
            device_id=mate, device_id_type=MESH,
        )

    def row_copy(j):
        target = {"row": ((z + 1 + j) % Z_CHIPS) * 2 + core, "sec": (sec + 1 + j // Z_CHIPS) % 2}
        return pltpu.make_async_remote_copy(
            src_ref=to_row.at[j], dst_ref=from_row.at[j], send_sem=row_send.at[j], recv_sem=row_recv.at[j],
            device_id=target, device_id_type=MESH,
        )

    def owner_of(i, owner_core):
        return ((z + 1 + i) % Z_CHIPS) * 4 + owner_core * 2 + (sec + 1 + i // Z_CHIPS) % 2

    def forward(j):
        mate_copy(j).wait_recv()
        to_row[j] = (mine[j] + from_mate[j]).astype(BF16)
        row_copy(j).start()

    tile_copy.wait()
    gather(listed_mate, owner_of(0, 1 - core))
    to_mate[0] = packed_gram(listed_mate)
    gather(listed_mine, owner_of(1, 1 - core))
    mate_copy(0).start()
    to_mate[1] = packed_gram(listed_mine)
    gather(listed_mine, owner_of(0, core))
    gather(listed_mate, owner_of(2, 1 - core))
    mate_copy(1).start()

    def gram_step(i):
        mine[i] = packed_gram(listed_mine)
        gather(listed_mine, owner_of(i + 1, core))
        to_mate[i + 2] = packed_gram(listed_mate)
        gather(listed_mate, owner_of(i + 3, 1 - core))
        mate_copy(i + 2).start()
        forward(i)

    pl.loop(0, 3)(gram_step)
    shifts[1].wait()

    @pl.loop(0, STEPS)
    def _(i):
        load(2, i).wait()
        for j in range(GROUP):
            wide[:, pl.ds(j * CHI, CHI)] = dot(edge[i * GROUP + j], from_right[...]).astype(BF16)
        right_sum[...] += dot(wide[...], proj_right[pl.ds(i * GROUP, GROUP)].reshape(GROUP * CHI, CHI))

    corner_copy(1).start()
    pl.loop(3, 6)(gram_step)
    corner_copy(0).wait()
    left_sum[...] = normalized(left_sum[...] + left_other[...])
    result(0).start()
    mine[6] = packed_gram(listed_mine)
    gather(listed_mate, owner_of(7, core))
    forward(6)
    mine[7] = packed_gram(listed_mate)
    mate_copy(7).wait_recv()
    total = mine[7] + from_mate[7]
    for j in range(7):
        row_copy(j).wait_recv()
        total = total + from_row[j].astype(F32)
    gram_sum[...] = unpack(total)
    result(2).start()
    corner_copy(1).wait()
    right_sum[...] = normalized(right_sum[...] + right_other[...])
    result(1).start()
    for i in range(2 * Z_CHIPS):
        mate_copy(i).wait_send()
    for j in range(7):
        row_copy(j).wait_send()
    for k in range(3):
        result(k).wait()


def column(sector_owner, row_order, block_size, block_sector, corner_left, corner_right, edge, proj_left, proj_right):
    hbm = pl.BlockSpec(memory_space=pltpu.HBM)
    square = jax.ShapeDtypeStruct((CHI, CHI), F32)
    whole = pltpu.VMEM((UNITS, CHI, CHI), BF16)
    dma = pltpu.SemaphoreType.DMA
    return pl.pallas_call(
        column_kernel,
        in_specs=[pl.BlockSpec(memory_space=pltpu.SMEM)] + [hbm] * 8,
        out_specs=(hbm, hbm, hbm),
        out_shape=(square, square, square),
        scratch_shapes=[
            pltpu.VMEM((1, UNITS * CHI), jnp.int32),
            pltpu.VMEM((1, LANES), jnp.int32),
            pltpu.VMEM((1, LANES), jnp.int32),
            pltpu.VMEM((64, CHI), F32),
            pltpu.VMEM((OWNERS, CHI), jnp.int32),
            pltpu.SMEM((OWNERS, CHI), jnp.int32),
            pltpu.VMEM((CHI, CHI), BF16),
            pltpu.VMEM((CHI, CHI), BF16),
            whole, whole, whole, whole,
            pltpu.VMEM((CHI, GROUP * CHI), BF16),
            pltpu.VMEM((UNITS * TILES, TILE, CHI), BF16),
            pltpu.VMEM((CAP_TILES * TILE, CHI), BF16),
            pltpu.VMEM((CAP_TILES * TILE, CHI), BF16),
            pltpu.VMEM((CHI, CHI), F32), pltpu.VMEM((CHI, CHI), F32),
            pltpu.VMEM((CHI, CHI), F32), pltpu.VMEM((CHI, CHI), F32),
            pltpu.VMEM((CHI, CHI), F32),
            pltpu.VMEM((8, PACKED, HALF), F32),
            pltpu.VMEM((8, PACKED, HALF), F32),
            pltpu.VMEM((8, PACKED, HALF), F32),
            pltpu.VMEM((7, PACKED, HALF), BF16),
            pltpu.VMEM((7, PACKED, HALF), BF16),
            dma((3,)), dma, dma((2,)), dma((2,)),
            dma((3, STEPS)), dma((2,)), dma((2,)), dma((8,)), dma((8,)), dma((7,)), dma((7,)), dma((3,)),
        ],
        cost_estimate=pl.CostEstimate(flops=9 * 2 * 12800 * 65536, bytes_accessed=24 << 20, transcendentals=0),
        compiler_params=pltpu.CompilerParams(
            collective_id=0, has_side_effects=True, vmem_limit_bytes=58 * 1024 * 1024
        ),
    )(sector_owner, row_order, block_size, block_sector, corner_left, corner_right, edge, proj_left, proj_right)


def finish_kernel(*refs):
    held, load_sem, store_sem = refs[6:]
    loads = [pltpu.make_async_copy(refs[k], held.at[k], load_sem.at[k]) for k in range(3)]
    stores = [pltpu.make_async_copy(held.at[k], refs[3 + k], store_sem.at[k]) for k in range(3)]
    for copy in loads:
        copy.start()
    for k in range(3):
        loads[k].wait()
        stores[k].start()
    for copy in stores:
        copy.wait()


def finish(*results):
    hbm = pl.BlockSpec(memory_space=pltpu.HBM)
    square = jax.ShapeDtypeStruct((CHI, CHI), F32)
    return pl.pallas_call(
        finish_kernel,
        in_specs=[hbm] * 3,
        out_specs=(hbm,) * 3,
        out_shape=(square,) * 3,
        scratch_shapes=[
            pltpu.VMEM((3, CHI, CHI), F32), pltpu.SemaphoreType.DMA((3,)), pltpu.SemaphoreType.DMA((3,)),
        ],
        compiler_params=pltpu.CompilerParams(vmem_limit_bytes=60 * 1024 * 1024),
    )(*results)


def body(
    corner_left, corner_right, edge_top, proj_left, proj_right, row_order, block_size, block_sector, sector_owner,
):
    sums = column(
        sector_owner,
        row_order.reshape(1, UNITS * CHI),
        block_size.reshape(1, LANES),
        block_sector.reshape(1, LANES),
        corner_left[0, 0],
        corner_right[0, 0],
        jnp.transpose(edge_top[0, 0], (1, 0, 2)),
        jnp.transpose(proj_left[0, 0], (1, 0, 2)),
        proj_right[0, 0],
    )
    return tuple(out[None, None] for out in finish(*sums))


def solution(mesh):
    in_specs = (
        P("col", "row", None, None),
        P("col", "row", None, None),
        P("col", "row", None, "sec", None),
        P("col", "row", None, "sec", None),
        P("col", "row", "sec", None, None),
        P("col", "row", "sec", None),
        P("col", "row", "sec", None),
        P("col", "row", "sec", None, None),
        P(),
    )
    out_specs = (
        P("col", "row", None, None),
        P("col", "row", None, None),
        P("col", ("row", "sec"), None, None),
    )
    return jax.shard_map(body, mesh=mesh, in_specs=in_specs, out_specs=out_specs, check_vma=False)
```
